512 devices in a mesh: dp: 16 (over z, core), table: 32 (over y, x).
Axes of the slice: x: 4, y: 8, z: 8, core: 2. Of those that a mesh axis runs over, the one named last changes fastest.
Arguments:
- events: bfloat16 [262144, 512], P(('dp', 'table')), may hold values from -6 to 6
- upstream: bfloat16 [262144, 512], P(('dp', 'table')), may hold values from -24 to 24
- w_in: bfloat16 [512, 2048], replicated, may hold values from -0.25 to 0.25
- w_out: bfloat16 [512, 512], replicated, may hold values from -0.25 to 0.25
- lengths: int32 [512, 8], P(('dp', 'table')), may hold values from 1 to 256, 512 in all within a row
- owners: int32 [262144, 1], P(('dp', 'table')), may hold values from 0 to 511; in each aligned block of 512 rows (0 to 511, 512 to 1023, ...) at most 2 rows name the same one
- item_rows: int32 [262144], P(('dp', 'table')), may hold values from 0 to 1023
Outputs:
- out_grad: float32 [512, 512], P('table', 'dp')
- table_grad: bfloat16 [524288, 512], P(('dp', 'table'))
The draws below stay inside these ranges and needn't reach their ends.
Inputs may be any that keep to these rules, and one draw needn't show every extreme that they name: Each device's lengths sum to 512; each is 1 to 256 and one of them equals 256. `owners`: among the 512 events of one device at most 2 name the same owner, and in some device some owner is named exactly 2 times.
All inputs are finite; a program needn't handle non-finite values.
Results may differ from the reference program's by a relative error of at most 0.0086.
Values may be sent and summed in bfloat16 or wider, within the bound.
A program may use at most 128 MiB of HBM per device.

```python
import math
import jax
import jax.numpy as jnp
import numpy as np
from jax import lax

D = 512
HEADS = 8
TOK_DEV = 512
USERS_DEV = 8
ROWS_DEV = 1024
CAP = 2
TOKENS = 262144
ROWS = 524288
DEVICES = 512


def with_ends(result, key, smallest, high):
    index_at = [jax.random.randint(jax.random.fold_in(key, axis), (), 0, length) for axis, length in enumerate(result.shape)]
    longest = result.shape.index(max(result.shape))
    beside = index_at[:longest] + [(index_at[longest] + 1) % result.shape[longest]] + index_at[longest + 1:]
    return result.at[tuple(index_at)].set(smallest).at[tuple(beside)].set(high)


def with_spikes(drawn, key, source, target, shards_of, factor):
    owner, partner = [(jnp.arange(drawn.shape[dim]) // (drawn.shape[dim] // shards_of)).reshape([-1 if axis == dim else 1 for axis in range(drawn.ndim)]) for dim in (source, target)]
    chosen = jax.random.permutation(key, shards_of)[partner]
    strong = (owner == chosen) | (owner == (partner + shards_of // 2) % shards_of)
    return jnp.where(strong, factor * drawn, drawn)


def shard_levels(stream_key, dims, cuts, smallest, largest):
    factor_of = 1.0
    for dim, shards_of in cuts:
        heights = jax.random.uniform(jax.random.fold_in(jax.random.fold_in(stream_key, 6), dim), (shards_of,), jnp.float32, smallest / len(cuts), largest / len(cuts))
        factor_of = factor_of * jnp.repeat(jnp.exp(heights), dims[dim] // shards_of).reshape((-1,) + (1,) * (len(dims) - 1 - dim))
    return factor_of


def rank_bounds(amount, lean):
    weights = [(1 << 20) // math.isqrt(grade ** lean) + 1 for grade in range(1, amount + 1)]
    spread = 1 + sum(weights) // (1 << 30)
    return np.cumsum(np.array([max(1, weight // spread) for weight in weights]))


def ranked_ids(stream_key, dims, amount, skew):
    grid = rank_bounds(amount, skew)
    ticket = jax.random.randint(jax.random.fold_in(stream_key, 1), dims, 0, int(grid[amount - 1]))
    rank = jnp.searchsorted(jnp.asarray(grid, jnp.int32), ticket, side="right")
    return jax.random.permutation(jax.random.fold_in(stream_key, 2), amount)[rank].astype(jnp.int32)


def split_up(count, total, limit, skew):
    loads = [(1 << 20) // math.isqrt(grade ** skew) + 1 for grade in range(2, count + 1)]
    surplus, given = total - limit - (count - 1), [1] * (count - 1)
    while surplus > 0:
        free = [i for i in range(count - 1) if given[i] < limit]
        pool, budget = sum([loads[i] for i in free]), surplus
        for i in free:
            addition = min(limit - given[i], max(1, budget * loads[i] // pool), surplus)
            given[i] = given[i] + addition
            surplus = surplus - addition
    return np.array([limit] + given)


def ragged(key, number_of, total, bound, lean):
    if number_of == 2:
        one = jax.random.randint(key, (), max(1, total - bound), min(bound, total - 1) + 1)
        return jnp.stack([one, total - one])
    sizes = jnp.asarray(split_up(number_of, total, bound, lean), jnp.int32)
    pairs = (number_of - 1) // 2
    giver, sink = sizes[1:1 + 2 * pairs:2], sizes[2:2 + 2 * pairs:2]
    slack = jnp.minimum(giver - 1, bound - sink)
    passed = jax.random.randint(jax.random.fold_in(key, 1), (pairs,), 0, 1 << 20) % (slack + 1)
    sizes = sizes.at[1:1 + 2 * pairs:2].set(giver - passed).at[2:2 + 2 * pairs:2].set(sink + passed)
    return sizes[jax.random.permutation(jax.random.fold_in(key, 2), number_of)]


def routed_block(stream_key, own, number, rows, number_of, top, most, slope):
    ranking = jax.random.permutation(stream_key, number_of)
    crowded, ordinary = load_shares(number_of, rows * top, most, slope, True), load_shares(number_of, rows * top, most, slope, False)
    places = jnp.arange(number_of)

    def named(sizes, offset_by):
        used = int((sizes > 0).sum())
        fixed = max(1, used // 4)
        moved = fixed + (places - fixed + offset_by * (used - fixed)) % max(1, number_of - fixed)
        return jnp.zeros((number_of,), jnp.int32).at[ranking[jnp.where(places < fixed, places, moved)]].set(jnp.asarray(sizes, jnp.int32))

    sizes = jnp.where(number % 4 == 0, named(crowded, number // 4), named(ordinary, number - number // 4 - 1))
    mixed = jax.random.permutation(jax.random.fold_in(own, 3), number_of)
    donor, sink = mixed[0:number_of // 2 * 2:2], mixed[1:number_of // 2 * 2:2]
    room = jnp.minimum(sizes[donor] - 1, most - sizes[sink]) // 2
    room = jnp.where((donor == ranking[0]) | (sink == ranking[0]) | (sizes[sink] == 0), 0, jnp.maximum(room, 0))
    moved = jax.random.randint(jax.random.fold_in(own, 4), (number_of // 2,), 0, 1 << 20) % (room + 1)
    sizes = sizes.at[donor].add(-moved).at[sink].add(moved)
    labels = jnp.searchsorted(jnp.cumsum(sizes), jnp.arange(rows * top), side="right").astype(jnp.int32)
    grid = labels.reshape(top, rows).T
    grid = grid[jax.random.permutation(jax.random.fold_in(own, 1), rows)]
    offset_by = jax.random.randint(jax.random.fold_in(own, 2), (rows, 1), 0, top)
    return jnp.take_along_axis(grid, (jnp.arange(top)[None, :] + offset_by) % top, axis=1)


def load_shares(amount, total, limit, skew, full):
    weights = [(1 << 20) // math.isqrt(standing ** skew) + 1 for standing in range(1, amount + 1)]
    largest = limit if full else min(limit, max(-(-total // amount), total * weights[0] // sum(weights)))
    least = 1 if total - largest >= amount - 1 else 0
    counts, spare = [largest] + [least] * (amount - 1), total - largest - least * (amount - 1)
    while spare > 0:
        candidates = [i for i in range(1, amount) if counts[i] < largest] or [i for i in range(1, amount) if counts[i] < limit]
        whole, remaining = sum([weights[i] for i in candidates]), spare
        for i in candidates:
            extra = min(limit - counts[i], max(1, remaining * weights[i] // whole), spare)
            counts[i] = counts[i] + extra
            spare = spare - extra
    return np.array(counts)


def normal_values(own_key, shape, deviation, most, cuts=(), kind=jnp.bfloat16):
    level = shard_levels(own_key, shape, cuts, -0.22, 0.18) if cuts else 1.0
    values = jax.random.normal(own_key, shape, jnp.float32) * deviation * level
    return jnp.minimum(jnp.maximum(values, -most), most).astype(kind)


def heavy_noise(rng, shape, scale, bound, shards, heavy, kind=jnp.bfloat16):
    array = scale * jax.random.normal(rng, shape, jnp.float32)
    if shards:
        array = array * shard_levels(rng, shape, shards, -0.22, 0.18)
    return jnp.clip(with_spikes(array, jax.random.fold_in(rng, 3), *heavy), -bound, bound).astype(kind)


def setup_inputs(seed: int = 0) -> dict:
    key_of = jax.random.split(jax.random.key(seed), 8)
    events = normal_values(key_of[0], (TOKENS, D), 1.0, 6.0, ((0, 512),))
    upstream = heavy_noise(key_of[1], (TOKENS, D), 1.0, 24.0, ((0, 512),), (0, 1, 512, 6.0))
    w_in = normal_values(key_of[2], (D, 4 * D), D ** -0.5, 0.25)
    w_out = normal_values(key_of[3], (D, D), D ** -0.5, 0.25)
    lengths = jax.vmap(lambda own: ragged(own, USERS_DEV, TOK_DEV, TOK_DEV // 2, 2))(jax.random.split(key_of[4], DEVICES)).reshape((DEVICES, USERS_DEV)).astype(jnp.int32)
    owners_keys = jax.random.split(jax.random.fold_in(key_of[5], 1), TOKENS // TOK_DEV)
    owners_turns = jax.random.permutation(jax.random.fold_in(key_of[5], 3), TOKENS // TOK_DEV)
    owners = jax.vmap(lambda own, number: routed_block(jax.random.fold_in(key_of[5], 2), own, number, TOK_DEV, DEVICES, 1, CAP, 2))(owners_keys, owners_turns).reshape((TOKENS, 1))
    item_rows = with_ends(ranked_ids(key_of[6], (TOKENS,), ROWS_DEV, 2), jax.random.fold_in(key_of[6], 3), 0, ROWS_DEV - 1).astype(jnp.int32)
    return {"events": events, "upstream": upstream, "w_in": w_in, "w_out": w_out, "lengths": lengths, "owners": owners, "item_rows": item_rows}


eps = 1e-06

def normalize(values):
    mean = lax.optimization_barrier(jnp.mean(values, axis=-1, keepdims=True))
    centered = values - mean
    inverse = lax.rsqrt(lax.optimization_barrier(jnp.mean(centered * centered, axis=-1, keepdims=True)) + eps)
    return (centered * inverse, inverse)

def norm_back(grad, normed, inverse):
    first = lax.optimization_barrier(jnp.mean(grad, axis=-1, keepdims=True))
    second = lax.optimization_barrier(jnp.mean(grad * normed, axis=-1, keepdims=True))
    return inverse * (grad - first - normed * second)

def silu_slope(values):
    sig = jax.nn.sigmoid(values)
    return sig * (1.0 + values * (1.0 - sig))

def segment_mask(lengths_row, count):
    ends = jnp.cumsum(lengths_row.astype(jnp.int32))
    place = jnp.arange(count, dtype=jnp.int32)
    segment = lax.optimization_barrier(jnp.sum((place[:, None] >= ends[None, :]).astype(jnp.int32), axis=1))
    same = segment[:, None] == segment[None, :]
    causal = place[None, :] <= place[:, None]
    return jnp.where(same & causal, 1.0 / 64.0, 0.0).astype(jnp.float32)

def layer_grads(events, upstream, w_in, w_out, lengths_row):
    count, width = events.shape
    head_dim = width // HEADS
    scale = 1.0 / math_sqrt(head_dim)
    x_norm, x_inv = normalize(events.astype(jnp.float32))
    normed = x_norm.astype(jnp.bfloat16)
    z_pre = jnp.dot(normed, w_in, preferred_element_type=jnp.float32)
    act = jax.nn.silu(z_pre).astype(jnp.bfloat16)
    u_part, v_part, q_part, k_part = jnp.split(act, 4, axis=1)
    mask = segment_mask(lengths_row, count)
    q_heads = q_part.reshape(count, HEADS, head_dim).astype(jnp.float32)
    k_heads = k_part.reshape(count, HEADS, head_dim).astype(jnp.float32)
    v_heads = v_part.reshape(count, HEADS, head_dim).astype(jnp.float32)
    scores = jnp.einsum('qhd,khd->hqk', q_heads, k_heads) * scale
    weights = (jax.nn.silu(scores) * mask[None]).astype(jnp.bfloat16)
    weights_f = weights.astype(jnp.float32)
    attended = jnp.einsum('hqk,khd->qhd', weights_f, v_heads).reshape(count, width)
    att_norm, att_inv = normalize(attended)
    u_float = u_part.astype(jnp.float32)
    gated = (att_norm * u_float).astype(jnp.bfloat16)
    gated_grad = jnp.dot(upstream, w_out.T, preferred_element_type=jnp.float32)
    u_grad = gated_grad * att_norm
    att_grad = norm_back(gated_grad * u_float, att_norm, att_inv).astype(jnp.bfloat16)
    att_heads = att_grad.reshape(count, HEADS, head_dim).astype(jnp.float32)
    weight_grad = jnp.einsum('qhd,khd->hqk', att_heads, v_heads)
    v_grad = jnp.einsum('hqk,qhd->khd', weights_f, att_heads)
    score_grad = (weight_grad * mask[None] * silu_slope(scores) * scale).astype(jnp.bfloat16)
    score_f = score_grad.astype(jnp.float32)
    q_grad = jnp.einsum('hqk,khd->qhd', score_f, k_heads)
    k_grad = jnp.einsum('hqk,qhd->khd', score_f, q_heads)
    joined = jnp.concatenate([u_grad, v_grad.reshape(count, width), q_grad.reshape(count, width), k_grad.reshape(count, width)], axis=1)
    z_grad = (joined * silu_slope(z_pre)).astype(jnp.bfloat16)
    normed_grad = jnp.dot(z_grad, w_in.T, preferred_element_type=jnp.float32)
    event_grad = (upstream.astype(jnp.float32) + norm_back(normed_grad, x_norm, x_inv)).astype(jnp.bfloat16)
    return (gated, event_grad)

def math_sqrt(value):
    return float(value) ** 0.5

def reference(events, upstream, w_in, w_out, lengths, owners, item_rows):
    devices = lengths.shape[0]
    event_blocks = events.reshape(devices, -1, D)
    upstream_blocks = upstream.reshape(devices, -1, D)

    def one_device(total, pieces):
        block_events, block_upstream, block_lengths = pieces
        gated, event_grad = layer_grads(block_events, block_upstream, w_in, w_out, block_lengths)
        total = total + jnp.dot(gated.T, block_upstream, preferred_element_type=jnp.float32)
        return (total, event_grad)
    start = jnp.zeros((D, D), jnp.float32)
    out_grad, grads = lax.scan(one_device, start, (event_blocks, upstream_blocks, lengths))
    ids = (owners[:, 0] * ROWS_DEV + item_rows).astype(jnp.int32)
    summed = jax.ops.segment_sum(grads.reshape(-1, D).astype(jnp.float32), ids, num_segments=ROWS)
    return (out_grad, summed.astype(jnp.bfloat16))
```

```python
import functools
import jax
import jax.numpy as jnp
from jax import lax
from jax.experimental import pallas as pl
from jax.experimental.pallas import tpu as pltpu
from jax.sharding import PartitionSpec as P

HEADS = 8
HD = 64
TOK = 512
D = 512
EPS = 1e-6
F32 = jnp.float32
BF16 = jnp.bfloat16
JB = 128
OUT_OF_MASK = -1e30


def dot_nn(a, b):
    return lax.dot_general(a, b, (((1,), (0,)), ((), ())), preferred_element_type=F32)


def dot_nt(a, b):
    return lax.dot_general(a, b, (((1,), (1,)), ((), ())), preferred_element_type=F32)


def window(jb):
    lo = jb * JB
    return lo, min(TOK, -(-(lo + JB + 255) // 128) * 128)


def build_bias(len_ref, bias_ref):
    ends, total = [], 0
    for n in range(8):
        total = total + len_ref[0, n]
        ends.append(total)
    col = lax.broadcasted_iota(jnp.int32, (TOK, 1), 0)
    row = lax.broadcasted_iota(jnp.int32, (1, TOK), 1)
    seg_col = jnp.zeros((TOK, 1), jnp.int32)
    seg_row = jnp.zeros((1, TOK), jnp.int32)
    for n in range(8):
        seg_col = seg_col + (col >= ends[n]).astype(jnp.int32)
        seg_row = seg_row + (row >= ends[n]).astype(jnp.int32)
    for jb in range(TOK // JB):
        lo, hi = window(jb)
        keep = (seg_col[lo:lo + JB] == seg_row[:, lo:hi]) & (col[lo:lo + JB] <= row[:, lo:hi])
        bias_ref[lo:lo + JB, lo:hi] = jnp.where(keep, 0.0, OUT_OF_MASK)


def zero_corners(ref, lead):
    zeros = jnp.zeros(lead + (128, 128), ref.dtype)
    full = (slice(None),) * len(lead)
    ref[full + (slice(0, 128), slice(384, 512))] = zeros
    ref[full + (slice(128, 256), slice(0, 128))] = zeros
    ref[full + (slice(384, 512), slice(256, 384))] = zeros


def normalize_events(ev_ref, xnt_ref, normedt_ref, inv_ref):
    x = ev_ref[...].T.astype(F32)
    mean = jnp.mean(x, axis=0, keepdims=True)
    c = x - mean
    inv = lax.rsqrt(jnp.mean(c * c, axis=0, keepdims=True) + EPS)
    xn = c * inv
    xnt_ref[...] = xn
    normedt_ref[...] = xn.astype(BF16)
    inv_ref[...] = inv


def project(w_in_ref, normedt_ref, slope_ref, act_ref):
    for c in range(16):
        lo = c * 128
        wt = w_in_ref[:, lo:lo + 128].T
        half = dot_nn(wt, normedt_ref[...]) * 0.5
        t = jnp.tanh(half)
        p = 1.0 + t
        act = half * p
        slope_ref[lo:lo + 128, :] = p + act * (1.0 - t)
        act_ref[lo:lo + 128, :] = act.astype(BF16)


def natural(act_ref, nat_ref):
    nat_ref[:, 0:512] = act_ref[512:1024, :].T
    nat_ref[:, 512:1024] = act_ref[1536:2048, :].T


def head_pair_cols(nat_ref, base, pair):
    return nat_ref[:, pl.ds(pl.multiple_of(base + pair * 128, 128), 128)]


def attend_head(h, act_ref, bias_ref, w_ref, dsl_ref, att_ref):
    r = pl.multiple_of(h * HD, HD)
    qt = act_ref[pl.ds(1024 + r, HD), :] * 0.0625
    kt = act_ref[pl.ds(1536 + r, HD), :]
    vt = act_ref[pl.ds(512 + r, HD), :] * (1.0 / 64.0)
    k = kt.T
    for jb in range(TOK // JB):
        lo, hi = window(jb)
        half = dot_nn(k[lo:lo + JB], qt[:, lo:hi]) + bias_ref[lo:lo + JB, lo:hi]
        t = jnp.tanh(half)
        p = 1.0 + t
        w = half * p
        w_ref[h, lo:lo + JB, lo:hi] = w.astype(BF16)
        dsl_ref[h, lo:lo + JB, lo:hi] = p + w * (1.0 - t)
    att_ref[pl.ds(r, HD), 0:256] = dot_nn(vt[:, 0:256], w_ref[h, 0:256, 0:256])
    att_ref[pl.ds(r, HD), 256:512] = dot_nn(vt, w_ref[h, :, 256:512])


def norm_att(att_ref, ainv_ref, act_ref, gated_ref):
    a = att_ref[...]
    mean = jnp.mean(a, axis=0, keepdims=True)
    c = a - mean
    inv = lax.rsqrt(jnp.mean(c * c, axis=0, keepdims=True) + EPS)
    an = c * inv
    att_ref[...] = an
    ainv_ref[...] = inv
    gated_ref[...] = (an * act_ref[0:512, :].astype(F32)).astype(BF16)


def att_backward(w_out_ref, up_ref, att_ref, ainv_ref, act_ref, slope_ref, zg_ref, ag_ref):
    gg = dot_nt(w_out_ref[...], up_ref[...])
    an = att_ref[...]
    zg_ref[0:512, :] = (gg * an * slope_ref[0:512, :]).astype(BF16)
    g = gg * act_ref[0:512, :].astype(F32)
    first = jnp.mean(g, axis=0, keepdims=True)
    second = jnp.mean(g * an, axis=0, keepdims=True)
    ag_ref[...] = ((g - first - an * second) * (ainv_ref[...] * (1.0 / 128.0))).astype(BF16)


def backward_head(h, act_ref, ag_ref, w_ref, dsl_ref, ds_ref, slope_ref, zg_ref):
    r = pl.multiple_of(h * HD, HD)
    qt = act_ref[pl.ds(1024 + r, HD), :]
    kt = act_ref[pl.ds(1536 + r, HD), :]
    v = act_ref[pl.ds(512 + r, HD), :].T
    ag = ag_ref[pl.ds(r, HD), :]
    for jb in range(TOK // JB):
        lo, hi = window(jb)
        wg = dot_nn(v[lo:lo + JB], ag[:, lo:hi])
        ds_ref[lo:lo + JB, lo:hi] = (wg * dsl_ref[h, lo:lo + JB, lo:hi]).astype(BF16)
    vg0 = dot_nt(ag, w_ref[h, 0:256, :])
    vg1 = dot_nt(ag[:, 256:512], w_ref[h, 256:512, 256:512])
    zg_ref[pl.ds(512 + r, HD), 0:256] = (vg0 * 2.0 * slope_ref[pl.ds(512 + r, HD), 0:256]).astype(BF16)
    zg_ref[pl.ds(512 + r, HD), 256:512] = (vg1 * 2.0 * slope_ref[pl.ds(512 + r, HD), 256:512]).astype(BF16)
    qg0 = dot_nn(kt[:, 0:256], ds_ref[0:256, 0:256])
    qg1 = dot_nn(kt, ds_ref[:, 256:512])
    zg_ref[pl.ds(1024 + r, HD), 0:256] = (qg0 * 0.125 * slope_ref[pl.ds(1024 + r, HD), 0:256]).astype(BF16)
    zg_ref[pl.ds(1024 + r, HD), 256:512] = (qg1 * 0.125 * slope_ref[pl.ds(1024 + r, HD), 256:512]).astype(BF16)
    kg0 = dot_nt(qt, ds_ref[0:256, :])
    kg1 = dot_nt(qt[:, 256:512], ds_ref[256:512, 256:512])
    zg_ref[pl.ds(1536 + r, HD), 0:256] = (kg0 * 0.125 * slope_ref[pl.ds(1536 + r, HD), 0:256]).astype(BF16)
    zg_ref[pl.ds(1536 + r, HD), 256:512] = (kg1 * 0.125 * slope_ref[pl.ds(1536 + r, HD), 256:512]).astype(BF16)


def event_gradient(w_in_ref, zg_ref, up_ref, xnt_ref, inv_ref, eg_ref):
    ng = dot_nn(w_in_ref[...], zg_ref[...])
    xn = xnt_ref[...]
    first = jnp.mean(ng, axis=0, keepdims=True)
    second = jnp.mean(ng * xn, axis=0, keepdims=True)
    back = (ng - first - xn * second) * (inv_ref[...] * 0.5)
    eg_ref[...] = (up_ref[...].T.astype(F32) + back).astype(BF16)


MESH = pl.DeviceIdType.MESH
SLOTS = 1024
ROWS_DEV = 1024
CHUNKS = 4
CW = D // CHUNKS


def log2(n):
    return n.bit_length() - 1


def one_hot(rows, cols_of):
    at = lax.broadcasted_iota(jnp.int32, (rows, cols_of.shape[1]), 0)
    return jnp.where(at == cols_of, 1.0, 0.0).astype(BF16)


def start_all(axis, size, rows, src_ref, dst_ref, send_sem, recv_sem):
    me = lax.axis_index(axis)
    mine = pl.ds(pl.multiple_of(me * rows, rows), rows)
    pltpu.make_async_copy(src_ref.at[mine], dst_ref.at[mine], recv_sem).start()

    def send(k, carry):
        peer = lax.rem(me + k, size)
        pltpu.make_async_remote_copy(
            src_ref=src_ref.at[pl.ds(pl.multiple_of(peer * rows, rows), rows)],
            dst_ref=dst_ref.at[mine],
            send_sem=send_sem,
            recv_sem=recv_sem,
            device_id={axis: peer},
            device_id_type=MESH,
        ).start()
        return carry

    lax.fori_loop(1, size, send, 0)


def wait_bytes(ref, sem):
    pltpu.make_async_copy(ref, ref, sem).wait()


def route_slots(owner_ref, item_ref, n_dp, n_table, oh_a, oh_b, meta_ref):
    cap = SLOTS // (n_dp * n_table)
    row = owner_ref[...]
    col = jnp.broadcast_to(row, (128, TOK)).T[:, 0:1]
    place_col = lax.broadcasted_iota(jnp.int32, (TOK, 1), 0)
    place_row = lax.broadcasted_iota(jnp.int32, (1, TOK), 1)
    earlier = (col == row) & (place_col < place_row)
    rank = jnp.sum(jnp.where(earlier, 1.0, 0.0), axis=0, keepdims=True).astype(jnp.int32)
    table, dp = row & (n_table - 1), row >> log2(n_table)
    oh_a[...] = one_hot(SLOTS, table * (n_dp * cap) + dp * cap + rank)
    oh_b[...] = one_hot(SLOTS, dp * (n_table * cap) + table * cap + rank)
    code = item_ref[...] + 1
    line = lax.broadcasted_iota(jnp.int32, (128, TOK), 0)
    high, low = (code >> 5).astype(F32), (code & 31).astype(F32)
    meta_t = jnp.where(line == 0, high, jnp.where(line == 1, low, 0.0)).astype(BF16)
    meta_ref[...] = dot_nt(oh_a[...], meta_t).astype(BF16)


def build_swap(first, second, cap, ref):
    out = lax.broadcasted_iota(jnp.int32, (SLOTS, 1), 0)
    slot = out & (cap - 1)
    a = (out >> log2(cap)) & (first - 1)
    b = out >> (log2(cap) + log2(first))
    at = lax.broadcasted_iota(jnp.int32, (SLOTS, SLOTS), 1)
    ref[...] = jnp.where(at == a * (second * cap) + b * cap + slot, 1.0, 0.0).astype(BF16)


def build_hits(meta, ref):
    lines = meta.astype(F32).T
    item = (lines[0:1] * 32.0 + lines[1:2] - 1.0).astype(jnp.int32)
    ref[...] = one_hot(ROWS_DEV, item)


def kernel(n_dp, n_table, *refs):
    names = INPUTS + OUTPUTS + tuple(scratch(n_dp, n_table))
    r = dict(zip(names, refs))
    ns = type("Refs", (), r)
    dp, table = lax.axis_index("dp"), lax.axis_index("table")
    core = lax.rem(dp, 2)
    cap = SLOTS // (n_dp * n_table)
    row_share, col_share, half_dp = D // n_table, D // n_dp, n_dp // 2

    barrier = pltpu.get_barrier_semaphore()
    for axis, size, me in (("table", n_table, table), ("dp", n_dp, dp)):
        def greet(k, carry, axis=axis, size=size, me=me):
            pl.semaphore_signal(
                barrier, inc=1, device_id={axis: lax.rem(me + k, size)}, device_id_type=MESH
            )
            return carry
        lax.fori_loop(1, size, greet, 0)

    route_slots(ns.owners, ns.items, n_dp, n_table, ns.oh_a, ns.oh_b, ns.meta.at[0])
    pl.semaphore_wait(barrier, n_table + n_dp - 2)
    start_all("table", n_table, n_dp * cap, ns.meta.at[0], ns.meta.at[1], ns.send.at[0], ns.recv.at[0])

    build_bias(ns.lengths, ns.bias)
    zero_corners(ns.w, (HEADS,))
    zero_corners(ns.ds, ())
    build_swap(n_table, n_dp, cap, ns.swap_a)
    build_swap(n_dp, n_table, cap, ns.swap_b)
    normalize_events(ns.events, ns.xnt, ns.normedt, ns.inv)
    project(ns.w_in, ns.normedt, ns.slope, ns.act)

    wait_bytes(ns.meta.at[1], ns.recv.at[0])
    ns.meta[2] = dot_nn(ns.swap_a[...], ns.meta[1]).astype(BF16)
    start_all("dp", n_dp, n_table * cap, ns.meta.at[2], ns.meta.at[3], ns.send.at[1], ns.recv.at[1])

    for h in range(HEADS):
        attend_head(h, ns.act, ns.bias, ns.w, ns.dsl, ns.att)
    norm_att(ns.att, ns.ainv, ns.act, ns.gated)
    for half in range(2):
        ns.part[half] = dot_nn(ns.gated[...], ns.upstream[:, half * 256:half * 256 + 256])
    to_core = pltpu.make_async_remote_copy(
        src_ref=ns.part.at[1 - core],
        dst_ref=ns.other,
        send_sem=ns.send.at[2],
        recv_sem=ns.recv.at[2],
        device_id={"dp": dp + 1 - 2 * core},
        device_id_type=MESH,
    )
    to_core.start()
    att_backward(ns.w_out, ns.upstream, ns.att, ns.ainv, ns.act, ns.slope, ns.zg, ns.ag)
    to_core.wait_recv()
    ns.rs_send[...] = (ns.part[core] + ns.other[...]).astype(BF16)
    start_all("table", n_table, row_share, ns.rs_send, ns.rs_recv, ns.send.at[3], ns.recv.at[3])

    for h in range(HEADS):
        backward_head(h, ns.act, ns.ag, ns.w, ns.dsl, ns.ds, ns.slope, ns.zg)

    event_gradient(ns.w_in, ns.zg, ns.upstream, ns.xnt, ns.inv, ns.eg)
    first = (("table", n_table, n_dp * cap, ns.oh_a), ("dp", n_dp, n_table * cap, ns.oh_b))
    second = (("dp", n_dp, n_table * cap, ns.swap_a), ("table", n_table, n_dp * cap, ns.swap_b))
    for q in range(CHUNKS):
        axis, size, rows, oh = first[q % 2]
        ns.moved[q, 0] = dot_nt(oh[...], ns.eg[q * CW:q * CW + CW, :]).astype(BF16)
        start_all(axis, size, rows, ns.moved.at[q, 0], ns.moved.at[q, 1], ns.send.at[5 + q], ns.recv.at[5 + q])

    wait_bytes(ns.rs_recv, ns.recv.at[3])
    share = ns.rs_recv[0:row_share].astype(F32)
    for t in range(1, n_table):
        share = share + ns.rs_recv[t * row_share:(t + 1) * row_share].astype(F32)
    for g in range(2):
        ns.fin_send[g] = share[:, g * 128:g * 128 + 128]
    z = dp // 2
    for m in range(half_dp):
        target = core * half_dp + m
        group = ns.fin_send.at[m * col_share // 128]

        @pl.when(target == dp)
        def _():
            pltpu.make_async_copy(group, ns.fin_recv.at[z], ns.recv.at[4]).start()

        @pl.when(target != dp)
        def _():
            pltpu.make_async_remote_copy(
                src_ref=group,
                dst_ref=ns.fin_recv.at[z],
                send_sem=ns.fin_sem.at[m],
                recv_sem=ns.recv.at[4],
                device_id={"dp": target},
                device_id_type=MESH,
            ).start()

    wait_bytes(ns.meta.at[3], ns.recv.at[1])
    build_hits(ns.meta[3], ns.hits_a)
    build_hits(dot_nn(ns.swap_b[...], ns.meta[3]), ns.hits_b)

    for q in range(CHUNKS):
        axis, size, rows, swap = second[q % 2]
        wait_bytes(ns.moved.at[q, 1], ns.recv.at[5 + q])
        ns.moved[q, 2] = dot_nn(swap[...], ns.moved[q, 1]).astype(BF16)
        start_all(axis, size, rows, ns.moved.at[q, 2], ns.moved.at[q, 3], ns.send.at[9 + q], ns.recv.at[9 + q])

    wait_bytes(ns.fin_recv, ns.recv.at[4])
    total = ns.fin_recv[0]
    for k in range(1, half_dp):
        total = total + ns.fin_recv[k]
    lane = lax.rem(lax.rem(dp, half_dp) * col_share, 128)
    block = total[:, 0:col_share]
    for at in range(col_share, 128, col_share):
        block = jnp.where(lane == at, total[:, at:at + col_share], block)
    ns.out_grad[...] = block

    for q in range(CHUNKS):
        wait_bytes(ns.moved.at[q, 3], ns.recv.at[9 + q])
        hits = (ns.hits_a, ns.hits_b)[q % 2]
        ns.table_grad[:, q * CW:q * CW + CW] = dot_nn(hits[...], ns.moved[q, 3]).astype(BF16)

    by_table, by_dp = pl.ds(0, (n_table - 1) * n_dp * cap), pl.ds(0, (n_dp - 1) * n_table * cap)
    wait_bytes(ns.meta.at[0, by_table], ns.send.at[0])
    wait_bytes(ns.meta.at[2, by_dp], ns.send.at[1])
    to_core.wait_send()
    wait_bytes(ns.rs_send.at[pl.ds(0, (n_table - 1) * row_share)], ns.send.at[3])
    for m in range(half_dp):
        target = core * half_dp + m

        @pl.when(target != dp)
        def _():
            wait_bytes(ns.fin_send.at[m * col_share // 128], ns.fin_sem.at[m])
    for q in range(CHUNKS):
        one, two = (by_table, by_dp) if q % 2 == 0 else (by_dp, by_table)
        wait_bytes(ns.moved.at[q, 0, one], ns.send.at[5 + q])
        wait_bytes(ns.moved.at[q, 2, two], ns.send.at[9 + q])


INPUTS = ("events", "upstream", "w_in", "w_out", "lengths", "owners", "items")
OUTPUTS = ("out_grad", "table_grad")


def scratch(n_dp, n_table):
    row_share = D // n_table
    vmem = pltpu.VMEM
    return dict(
        bias=vmem((TOK, TOK), F32),
        xnt=vmem((D, TOK), F32),
        normedt=vmem((D, TOK), BF16),
        inv=vmem((1, TOK), F32),
        slope=vmem((4 * D, TOK), F32),
        act=vmem((4 * D, TOK), BF16),
        w=vmem((HEADS, TOK, TOK), BF16),
        dsl=vmem((HEADS, TOK, TOK), F32),
        att=vmem((D, TOK), F32),
        ainv=vmem((1, TOK), F32),
        gated=vmem((D, TOK), BF16),
        zg=vmem((4 * D, TOK), BF16),
        ag=vmem((D, TOK), BF16),
        ds=vmem((TOK, TOK), BF16),
        eg=vmem((D, TOK), BF16),
        oh_a=vmem((SLOTS, TOK), BF16),
        oh_b=vmem((SLOTS, TOK), BF16),
        swap_a=vmem((SLOTS, SLOTS), BF16),
        swap_b=vmem((SLOTS, SLOTS), BF16),
        hits_a=vmem((ROWS_DEV, SLOTS), BF16),
        hits_b=vmem((ROWS_DEV, SLOTS), BF16),
        meta=vmem((4, SLOTS, 128), BF16),
        moved=vmem((CHUNKS, 4, SLOTS, CW), BF16),
        part=vmem((2, D, 256), F32),
        other=vmem((D, 256), F32),
        rs_send=vmem((D, 256), BF16),
        rs_recv=vmem((D, 256), BF16),
        fin_send=vmem((2, row_share, 128), F32),
        fin_recv=vmem((n_dp // 2, row_share, 128), F32),
        send=pltpu.SemaphoreType.DMA((5 + 2 * CHUNKS,)),
        recv=pltpu.SemaphoreType.DMA((5 + 2 * CHUNKS,)),
        fin_sem=pltpu.SemaphoreType.DMA((n_dp // 2,)),
    )


def solution(mesh):
    n_dp, n_table = mesh.shape["dp"], mesh.shape["table"]
    in_vmem = pl.BlockSpec(memory_space=pltpu.VMEM)
    in_smem = pl.BlockSpec(memory_space=pltpu.SMEM)

    def local(events, upstream, w_in, w_out, lengths, owners, item_rows):
        return pl.pallas_call(
            functools.partial(kernel, n_dp, n_table),
            out_shape=(
                jax.ShapeDtypeStruct((D // n_table, D // n_dp), F32),
                jax.ShapeDtypeStruct((ROWS_DEV, D), BF16),
            ),
            in_specs=[in_vmem] * 4 + [in_smem] + [in_vmem] * 2,
            out_specs=(in_vmem, in_vmem),
            scratch_shapes=list(scratch(n_dp, n_table).values()),
            compiler_params=pltpu.CompilerParams(
                collective_id=0, has_side_effects=True, vmem_limit_bytes=60 << 20
            ),
        )(events, upstream, w_in, w_out, lengths, owners.reshape(1, TOK), item_rows.reshape(1, TOK))

    both = P(("dp", "table"), None)
    return jax.shard_map(
        local,
        mesh=mesh,
        in_specs=(both, both, P(), P(), both, both, P(("dp", "table"))),
        out_specs=(P("table", "dp"), both),
        check_vma=False,
    )
```

```python
import functools
import jax
import jax.numpy as jnp
from jax import lax
from jax.experimental import pallas as pl
from jax.experimental.pallas import tpu as pltpu
from jax.sharding import PartitionSpec as P

HEADS = 8
HD = 64
TOK = 512
D = 512
EPS = 1e-6
F32 = jnp.float32
BF16 = jnp.bfloat16
JB = 128
OUT_OF_MASK = -1e30


def dot_nn(a, b):
    return lax.dot_general(a, b, (((1,), (0,)), ((), ())), preferred_element_type=F32)


def dot_nt(a, b):
    return lax.dot_general(a, b, (((1,), (1,)), ((), ())), preferred_element_type=F32)


def window(jb):
    lo = jb * JB
    return lo, min(TOK, -(-(lo + JB + 255) // 128) * 128)


def build_bias(len_ref, bias_ref):
    ends, total = [], 0
    for n in range(8):
        total = total + len_ref[0, n]
        ends.append(total)
    col = lax.broadcasted_iota(jnp.int32, (TOK, 1), 0)
    row = lax.broadcasted_iota(jnp.int32, (1, TOK), 1)
    seg_col = jnp.zeros((TOK, 1), jnp.int32)
    seg_row = jnp.zeros((1, TOK), jnp.int32)
    for n in range(8):
        seg_col = seg_col + (col >= ends[n]).astype(jnp.int32)
        seg_row = seg_row + (row >= ends[n]).astype(jnp.int32)
    for jb in range(TOK // JB):
        lo, hi = window(jb)
        keep = (seg_col[lo:lo + JB] == seg_row[:, lo:hi]) & (col[lo:lo + JB] <= row[:, lo:hi])
        bias_ref[lo:lo + JB, lo:hi] = jnp.where(keep, 0.0, OUT_OF_MASK)


def zero_corners(ref, lead):
    zeros = jnp.zeros(lead + (128, 128), ref.dtype)
    full = (slice(None),) * len(lead)
    ref[full + (slice(0, 128), slice(384, 512))] = zeros
    ref[full + (slice(128, 256), slice(0, 128))] = zeros
    ref[full + (slice(384, 512), slice(256, 384))] = zeros


def normalize_events(ev_ref, xnt_ref, normedt_ref, inv_ref):
    x = ev_ref[...].T.astype(F32)
    mean = jnp.mean(x, axis=0, keepdims=True)
    c = x - mean
    inv = lax.rsqrt(jnp.mean(c * c, axis=0, keepdims=True) + EPS)
    xn = c * inv
    xnt_ref[...] = xn
    normedt_ref[...] = xn.astype(BF16)
    inv_ref[...] = inv


def project(w_in_ref, normedt_ref, slope_ref, act_ref):
    for c in range(16):
        lo = c * 128
        wt = w_in_ref[:, lo:lo + 128].T
        half = dot_nn(wt, normedt_ref[...]) * 0.5
        t = jnp.tanh(half)
        p = 1.0 + t
        act = half * p
        slope_ref[lo:lo + 128, :] = p + act * (1.0 - t)
        act_ref[lo:lo + 128, :] = act.astype(BF16)


def natural(act_ref, nat_ref):
    nat_ref[:, 0:512] = act_ref[512:1024, :].T
    nat_ref[:, 512:1024] = act_ref[1536:2048, :].T


def head_pair_cols(nat_ref, base, pair):
    return nat_ref[:, pl.ds(pl.multiple_of(base + pair * 128, 128), 128)]


def attend_head(h, act_ref, bias_ref, w_ref, dsl_ref, att_ref):
    r = pl.multiple_of(h * HD, HD)
    qt = act_ref[pl.ds(1024 + r, HD), :] * 0.0625
    kt = act_ref[pl.ds(1536 + r, HD), :]
    vt = act_ref[pl.ds(512 + r, HD), :] * (1.0 / 64.0)
    k = kt.T
    for jb in range(TOK // JB):
        lo, hi = window(jb)
        half = dot_nn(k[lo:lo + JB], qt[:, lo:hi]) + bias_ref[lo:lo + JB, lo:hi]
        t = jnp.tanh(half)
        p = 1.0 + t
        w = half * p
        w_ref[h, lo:lo + JB, lo:hi] = w.astype(BF16)
        dsl_ref[h, lo:lo + JB, lo:hi] = p + w * (1.0 - t)
    att_ref[pl.ds(r, HD), 0:256] = dot_nn(vt[:, 0:256], w_ref[h, 0:256, 0:256])
    att_ref[pl.ds(r, HD), 256:512] = dot_nn(vt, w_ref[h, :, 256:512])


def norm_att(att_ref, ainv_ref, act_ref, gated_ref):
    a = att_ref[...]
    mean = jnp.mean(a, axis=0, keepdims=True)
    c = a - mean
    inv = lax.rsqrt(jnp.mean(c * c, axis=0, keepdims=True) + EPS)
    an = c * inv
    att_ref[...] = an
    ainv_ref[...] = inv
    gated_ref[...] = (an * act_ref[0:512, :].astype(F32)).astype(BF16)


def att_backward(w_out_ref, up_ref, att_ref, ainv_ref, act_ref, slope_ref, zg_ref, ag_ref):
    gg = dot_nt(w_out_ref[...], up_ref[...])
    an = att_ref[...]
    zg_ref[0:512, :] = (gg * an * slope_ref[0:512, :]).astype(BF16)
    g = gg * act_ref[0:512, :].astype(F32)
    first = jnp.mean(g, axis=0, keepdims=True)
    second = jnp.mean(g * an, axis=0, keepdims=True)
    ag_ref[...] = ((g - first - an * second) * (ainv_ref[...] * (1.0 / 128.0))).astype(BF16)


def backward_head(h, act_ref, ag_ref, w_ref, dsl_ref, ds_ref, slope_ref, zg_ref):
    r = pl.multiple_of(h * HD, HD)
    qt = act_ref[pl.ds(1024 + r, HD), :]
    kt = act_ref[pl.ds(1536 + r, HD), :]
    v = act_ref[pl.ds(512 + r, HD), :].T
    ag = ag_ref[pl.ds(r, HD), :]
    for jb in range(TOK // JB):
        lo, hi = window(jb)
        wg = dot_nn(v[lo:lo + JB], ag[:, lo:hi])
        ds_ref[lo:lo + JB, lo:hi] = (wg * dsl_ref[h, lo:lo + JB, lo:hi]).astype(BF16)
    vg0 = dot_nt(ag, w_ref[h, 0:256, :])
    vg1 = dot_nt(ag[:, 256:512], w_ref[h, 256:512, 256:512])
    zg_ref[pl.ds(512 + r, HD), 0:256] = (vg0 * 2.0 * slope_ref[pl.ds(512 + r, HD), 0:256]).astype(BF16)
    zg_ref[pl.ds(512 + r, HD), 256:512] = (vg1 * 2.0 * slope_ref[pl.ds(512 + r, HD), 256:512]).astype(BF16)
    qg0 = dot_nn(kt[:, 0:256], ds_ref[0:256, 0:256])
    qg1 = dot_nn(kt, ds_ref[:, 256:512])
    zg_ref[pl.ds(1024 + r, HD), 0:256] = (qg0 * 0.125 * slope_ref[pl.ds(1024 + r, HD), 0:256]).astype(BF16)
    zg_ref[pl.ds(1024 + r, HD), 256:512] = (qg1 * 0.125 * slope_ref[pl.ds(1024 + r, HD), 256:512]).astype(BF16)
    kg0 = dot_nt(qt, ds_ref[0:256, :])
    kg1 = dot_nt(qt[:, 256:512], ds_ref[256:512, 256:512])
    zg_ref[pl.ds(1536 + r, HD), 0:256] = (kg0 * 0.125 * slope_ref[pl.ds(1536 + r, HD), 0:256]).astype(BF16)
    zg_ref[pl.ds(1536 + r, HD), 256:512] = (kg1 * 0.125 * slope_ref[pl.ds(1536 + r, HD), 256:512]).astype(BF16)


def event_gradient(w_in_ref, zg_ref, up_ref, xnt_ref, inv_ref, eg_ref):
    ng = dot_nn(w_in_ref[...], zg_ref[...])
    xn = xnt_ref[...]
    first = jnp.mean(ng, axis=0, keepdims=True)
    second = jnp.mean(ng * xn, axis=0, keepdims=True)
    back = (ng - first - xn * second) * (inv_ref[...] * 0.5)
    eg_ref[...] = (up_ref[...].T.astype(F32) + back).astype(BF16)


MESH = pl.DeviceIdType.MESH
SLOTS = 1024
ROWS_DEV = 1024


def log2(n):
    return n.bit_length() - 1


def one_hot(rows, cols_of):
    at = lax.broadcasted_iota(jnp.int32, (rows, cols_of.shape[1]), 0)
    return jnp.where(at == cols_of, 1.0, 0.0).astype(BF16)


def start_all(axis, size, rows, src_ref, dst_ref, send_sem, recv_sem, lo=0, step=1):
    at = lax.axis_index(axis)
    me = lax.div(at - lo, step)
    mine = pl.ds(pl.multiple_of(me * rows, rows), rows)
    pltpu.make_async_copy(src_ref.at[mine], dst_ref.at[mine], recv_sem).start()

    def send(k, carry):
        peer = lax.rem(me + k, size)
        pltpu.make_async_remote_copy(
            src_ref=src_ref.at[pl.ds(pl.multiple_of(peer * rows, rows), rows)],
            dst_ref=dst_ref.at[mine],
            send_sem=send_sem,
            recv_sem=recv_sem,
            device_id={axis: lo + peer * step},
            device_id_type=MESH,
        ).start()
        return carry

    lax.fori_loop(1, size, send, 0)


def wait_bytes(ref, sem):
    pltpu.make_async_copy(ref, ref, sem).wait()


def route_slots(owner_ref, item_ref, n_dp, n_table, oh_a, oh_b, meta_ref):
    pairs = n_dp * n_table
    cap = SLOTS // pairs
    row = owner_ref[...]
    col = jnp.broadcast_to(row, (128, TOK)).T[:, 0:1]
    place_col = lax.broadcasted_iota(jnp.int32, (TOK, 1), 0)
    place_row = lax.broadcasted_iota(jnp.int32, (1, TOK), 1)
    earlier = (col == row) & (place_col < place_row)
    rank = jnp.sum(jnp.where(earlier, 1.0, 0.0), axis=0, keepdims=True).astype(jnp.int32)
    table, dp = row & (n_table - 1), row >> log2(n_table)
    oh_a[...] = one_hot(SLOTS, table * (n_dp * cap) + dp * cap + rank)
    oh_b[...] = one_hot(SLOTS, dp * (n_table * cap) + table * cap + rank)
    code = item_ref[...] + 1
    line = lax.broadcasted_iota(jnp.int32, (128, TOK), 0)
    words = jnp.where((line & 1) == 0, code >> 5, code & 31).astype(F32)
    meta_t = jnp.where((line >> 1) == rank, words, 0.0).astype(BF16)
    meta_ref[...] = dot_nt(one_hot(pairs, table * n_dp + dp), meta_t).astype(BF16)


def swap_rows(first, second, cap):
    n = first * second * cap
    out = lax.broadcasted_iota(jnp.int32, (n, 1), 0)
    slot = out & (cap - 1)
    a = (out >> log2(cap)) & (first - 1)
    b = out >> (log2(cap) + log2(first))
    at = lax.broadcasted_iota(jnp.int32, (n, n), 1)
    return jnp.where(at == a * (second * cap) + b * cap + slot, 1.0, 0.0).astype(BF16)


def item_lanes(meta, n_dp, n_table):
    pairs = n_dp * n_table
    cap = SLOTS // pairs
    lines = meta.astype(F32).T.astype(BF16)
    col = lax.broadcasted_iota(jnp.int32, (1, SLOTS), 1)
    word = lax.broadcasted_iota(jnp.int32, (128, SLOTS), 0)
    slot, pair = col & (cap - 1), col >> log2(cap)
    other = (pair & (n_dp - 1)) * n_table + (pair >> log2(n_dp))
    items = []
    for order in (pair, other):
        spread = dot_nn(lines, one_hot(pairs, order))
        high = jnp.sum(jnp.where(word == 2 * slot, spread, 0.0), axis=0, keepdims=True)
        low = jnp.sum(jnp.where(word == 2 * slot + 1, spread, 0.0), axis=0, keepdims=True)
        items.append((high * 32.0 + low - 1.0).astype(jnp.int32))
    return items


def kernel(n_dp, n_table, *refs):
    names = INPUTS + OUTPUTS + tuple(scratch(n_dp, n_table))
    ns = type("Refs", (), dict(zip(names, refs)))
    dp, table = lax.axis_index("dp"), lax.axis_index("table")
    core = lax.rem(dp, 2)
    pairs = n_dp * n_table
    cap = SLOTS // pairs
    nx = 4
    ny = n_table // nx
    row_share, col_share, half_dp = D // n_table, D // n_dp, n_dp // 2
    x_rows = ny * row_share

    barrier = pltpu.get_barrier_semaphore()
    for axis, size, me in (("table", n_table, table), ("dp", n_dp, dp)):
        def greet(k, carry, axis=axis, size=size, me=me):
            pl.semaphore_signal(
                barrier, inc=1, device_id={axis: lax.rem(me + k, size)}, device_id_type=MESH
            )
            return carry
        lax.fori_loop(1, size, greet, 0)

    loads = {}
    for n, name in enumerate(("events", "w_in", "w_out", "upstream")):
        loads[name] = pltpu.make_async_copy(getattr(ns, name), getattr(ns, name + "_v"), ns.load.at[n])
        loads[name].start()

    route_slots(ns.owners, ns.items, n_dp, n_table, ns.oh_a, ns.oh_b, ns.meta.at[0])
    build_bias(ns.lengths, ns.bias)
    zero_corners(ns.w, (HEADS,))
    zero_corners(ns.ds, ())
    ns.swap_a[...] = swap_rows(n_table, n_dp, cap)
    ns.swap_b[...] = swap_rows(n_dp, n_table, cap)
    loads["events"].wait()
    normalize_events(ns.events_v, ns.xnt, ns.normedt, ns.inv)
    loads["w_in"].wait()
    project(ns.w_in_v, ns.normedt, ns.slope, ns.act)

    pl.semaphore_wait(barrier, n_table + n_dp - 2)
    start_all("table", n_table, n_dp, ns.meta.at[0], ns.meta.at[1], ns.send.at[0], ns.recv.at[0])

    for h in range(HEADS):
        attend_head(h, ns.act, ns.bias, ns.w, ns.dsl, ns.att)
    norm_att(ns.att, ns.ainv, ns.act, ns.gated)
    loads["upstream"].wait()
    for half in range(2):
        ns.part[half] = dot_nn(ns.gated[...], ns.upstream_v[:, half * 256:half * 256 + 256])
    to_core = pltpu.make_async_remote_copy(
        src_ref=ns.part.at[1 - core],
        dst_ref=ns.other,
        send_sem=ns.send.at[2],
        recv_sem=ns.recv.at[2],
        device_id={"dp": dp + 1 - 2 * core},
        device_id_type=MESH,
    )
    to_core.start()
    loads["w_out"].wait()
    att_backward(ns.w_out_v, ns.upstream_v, ns.att, ns.ainv, ns.act, ns.slope, ns.zg, ns.ag)

    def backward(lo, hi):
        for h in range(lo, hi):
            backward_head(h, ns.act, ns.ag, ns.w, ns.dsl, ns.ds, ns.slope, ns.zg)

    backward(0, 2)
    to_core.wait_recv()
    for t in range(n_table):
        y, x = t // nx, t % nx
        rows = slice(t * row_share, (t + 1) * row_share)
        ns.x_send[x * x_rows + y * row_share:x * x_rows + (y + 1) * row_share] = (
            ns.part[core, rows] + ns.other[rows]
        ).astype(BF16)
    start_all("table", nx, x_rows, ns.x_send, ns.x_recv, ns.send.at[3], ns.recv.at[3], lo=lax.div(table, nx) * nx)
    wait_bytes(ns.meta.at[1], ns.recv.at[0])
    ns.meta[2] = dot_nn(swap_rows(n_table, n_dp, 1), ns.meta[1]).astype(BF16)
    start_all("dp", n_dp, n_table, ns.meta.at[2], ns.meta.at[3], ns.send.at[1], ns.recv.at[1])
    backward(2, 7)
    wait_bytes(ns.x_recv, ns.recv.at[3])
    share = ns.x_recv[0:x_rows].astype(F32)
    for x in range(1, nx):
        share = share + ns.x_recv[x * x_rows:(x + 1) * x_rows].astype(F32)
    ns.y_send[...] = share.astype(BF16)
    start_all("table", ny, row_share, ns.y_send, ns.y_recv, ns.send.at[4], ns.recv.at[4], lo=lax.rem(table, nx), step=nx)
    backward(7, 8)

    event_gradient(ns.w_in_v, ns.zg, ns.upstream_v, ns.xnt, ns.inv, ns.eg)
    first = (("table", n_table, n_dp * cap), ("dp", n_dp, n_table * cap))
    second = first[::-1]

    def hop_one(path, half):
        lanes = pl.ds(half * 128, 128)
        start_all(
            *first[path], ns.moved.at[path, :, lanes], ns.landed.at[path, half],
            ns.hop_send.at[path, half, 0], ns.hop_recv.at[path, half, 0],
        )

    ns.moved[0] = dot_nt(ns.oh_a[...], ns.eg[0:256, :]).astype(BF16)
    hop_one(0, 0)
    ns.moved[1] = dot_nt(ns.oh_b[...], ns.eg[256:512, :]).astype(BF16)
    hop_one(1, 0)
    hop_one(0, 1)
    hop_one(1, 1)

    wait_bytes(ns.y_recv, ns.recv.at[4])
    share = ns.y_recv[0:row_share].astype(F32)
    for y in range(1, ny):
        share = share + ns.y_recv[y * row_share:(y + 1) * row_share].astype(F32)
    for g in range(2):
        ns.fin_send[g] = share[:, g * 128:g * 128 + 128]
    z = lax.div(dp, 2)
    for m in range(half_dp):
        target = core * half_dp + m
        group = ns.fin_send.at[m * col_share // 128]

        @pl.when(target == dp)
        def _():
            pltpu.make_async_copy(group, ns.fin_recv.at[z], ns.recv.at[5]).start()

        @pl.when(target != dp)
        def _():
            pltpu.make_async_remote_copy(
                src_ref=group,
                dst_ref=ns.fin_recv.at[z],
                send_sem=ns.fin_sem.at[m],
                recv_sem=ns.recv.at[5],
                device_id={"dp": target},
                device_id_type=MESH,
            ).start()

    wait_bytes(ns.meta.at[3], ns.recv.at[1])
    items = item_lanes(ns.meta[3], n_dp, n_table)
    ns.item_rows[0:1, :] = items[0]
    ns.item_rows[1:2, :] = items[1]

    for half in range(2):
        for path, swap in ((0, ns.swap_a), (1, ns.swap_b)):
            wait_bytes(ns.landed.at[path, half], ns.hop_recv.at[path, half, 0])
            ns.again[path, half] = dot_nn(swap[...], ns.landed[path, half]).astype(BF16)
            start_all(
                *second[path], ns.again.at[path, half], ns.arrived.at[path, :, pl.ds(half * 128, 128)],
                ns.hop_send.at[path, half, 1], ns.hop_recv.at[path, half, 1],
            )

    wait_bytes(ns.fin_recv, ns.recv.at[5])
    total = ns.fin_recv[0]
    for k in range(1, half_dp):
        total = total + ns.fin_recv[k]
    lane = lax.rem(lax.rem(dp, half_dp) * col_share, 128)
    block = total[:, 0:col_share]
    for at in range(col_share, 128, col_share):
        block = jnp.where(lane == at, total[:, at:at + col_share], block)
    ns.grad_block[...] = block

    wait_bytes(ns.meta.at[0, pl.ds(0, (n_table - 1) * n_dp)], ns.send.at[0])
    wait_bytes(ns.meta.at[2, pl.ds(0, (n_dp - 1) * n_table)], ns.send.at[1])
    to_core.wait_send()
    wait_bytes(ns.x_send.at[pl.ds(0, (nx - 1) * x_rows)], ns.send.at[3])
    if ny > 1:
        wait_bytes(ns.y_send.at[pl.ds(0, (ny - 1) * row_share)], ns.send.at[4])
    for m in range(half_dp):
        target = core * half_dp + m

        @pl.when(target != dp)
        def _():
            wait_bytes(ns.fin_send.at[m * col_share // 128], ns.fin_sem.at[m])
    for half in range(2):
        for path in range(2):
            for hop, (_, size, rows) in enumerate((first[path], second[path])):
                wait_bytes(ns.again.at[path, half, pl.ds(0, (size - 1) * rows)], ns.hop_send.at[path, half, hop])
    for half in range(2):
        for path in range(2):
            wait_bytes(ns.arrived.at[path, :, pl.ds(half * 128, 128)], ns.hop_recv.at[path, half, 1])


def place_kernel(arrived_ref, item_ref, block_ref, out_ref, table_ref, rows, load):
    copies = [pltpu.make_async_copy(arrived_ref.at[p], rows.at[p], load.at[p]) for p in range(2)]
    for copy in copies:
        copy.start()
    out_ref[...] = block_ref[...]
    for p in range(2):
        hits = one_hot(ROWS_DEV, item_ref[p:p + 1, :])
        copies[p].wait()
        table_ref[:, p * 256:p * 256 + 256] = dot_nn(hits, rows[p]).astype(BF16)


INPUTS = ("events", "upstream", "w_in", "w_out", "lengths", "owners", "items")
OUTPUTS = ("grad_block", "item_rows", "arrived")


def scratch(n_dp, n_table):
    row_share = D // n_table
    pairs = n_dp * n_table
    vmem = pltpu.VMEM
    dma = pltpu.SemaphoreType.DMA
    return dict(
        events_v=vmem((TOK, D), BF16),
        upstream_v=vmem((TOK, D), BF16),
        w_in_v=vmem((D, 4 * D), BF16),
        w_out_v=vmem((D, D), BF16),
        bias=vmem((TOK, TOK), F32),
        xnt=vmem((D, TOK), F32),
        normedt=vmem((D, TOK), BF16),
        inv=vmem((1, TOK), F32),
        slope=vmem((4 * D, TOK), F32),
        act=vmem((4 * D, TOK), BF16),
        w=vmem((HEADS, TOK, TOK), BF16),
        dsl=vmem((HEADS, TOK, TOK), F32),
        att=vmem((D, TOK), F32),
        ainv=vmem((1, TOK), F32),
        gated=vmem((D, TOK), BF16),
        zg=vmem((4 * D, TOK), BF16),
        ag=vmem((D, TOK), BF16),
        ds=vmem((TOK, TOK), BF16),
        eg=vmem((D, TOK), BF16),
        oh_a=vmem((SLOTS, TOK), BF16),
        oh_b=vmem((SLOTS, TOK), BF16),
        swap_a=vmem((SLOTS, SLOTS), BF16),
        swap_b=vmem((SLOTS, SLOTS), BF16),
        meta=vmem((4, pairs, 128), BF16),
        moved=vmem((2, SLOTS, 256), BF16),
        landed=vmem((2, 2, SLOTS, 128), BF16),
        again=vmem((2, 2, SLOTS, 128), BF16),
        part=vmem((2, D, 256), F32),
        other=vmem((D, 256), F32),
        x_send=vmem((D, 256), BF16),
        x_recv=vmem((D, 256), BF16),
        y_send=vmem((D // 4, 256), BF16),
        y_recv=vmem((D // 4, 256), BF16),
        fin_send=vmem((2, row_share, 128), F32),
        fin_recv=vmem((n_dp // 2, row_share, 128), F32),
        load=dma((4,)),
        send=dma((6,)),
        recv=dma((6,)),
        hop_send=dma((2, 2, 2)),
        hop_recv=dma((2, 2, 2)),
        fin_sem=dma((n_dp // 2,)),
    )


def solution(mesh):
    n_dp, n_table = mesh.shape["dp"], mesh.shape["table"]
    in_vmem = pl.BlockSpec(memory_space=pltpu.VMEM)
    in_smem = pl.BlockSpec(memory_space=pltpu.SMEM)
    anywhere = pl.BlockSpec(memory_space=pl.ANY)

    def local(events, upstream, w_in, w_out, lengths, owners, item_rows):
        block = jax.ShapeDtypeStruct((D // n_table, D // n_dp), F32)
        grad_block, items, arrived = pl.pallas_call(
            functools.partial(kernel, n_dp, n_table),
            out_shape=(
                block,
                jax.ShapeDtypeStruct((8, SLOTS), jnp.int32),
                jax.ShapeDtypeStruct((2, SLOTS, 256), BF16),
            ),
            in_specs=[anywhere] * 4 + [in_smem] + [in_vmem] * 2,
            out_specs=(in_vmem, in_vmem, anywhere),
            scratch_shapes=list(scratch(n_dp, n_table).values()),
            compiler_params=pltpu.CompilerParams(
                collective_id=0, has_side_effects=True, vmem_limit_bytes=60 << 20
            ),
        )(events, upstream, w_in, w_out, lengths, owners.reshape(1, TOK), item_rows.reshape(1, TOK))
        return pl.pallas_call(
            place_kernel,
            out_shape=(block, jax.ShapeDtypeStruct((ROWS_DEV, D), BF16)),
            in_specs=[anywhere, in_vmem, in_vmem],
            out_specs=(in_vmem, in_vmem),
            scratch_shapes=[pltpu.VMEM((2, SLOTS, 256), BF16), pltpu.SemaphoreType.DMA((2,))],
            compiler_params=pltpu.CompilerParams(vmem_limit_bytes=60 << 20),
        )(arrived, items, grad_block)

    both = P(("dp", "table"), None)
    return jax.shard_map(
        local,
        mesh=mesh,
        in_specs=(both, both, P(), P(), both, both, P(("dp", "table"))),
        out_specs=(P("table", "dp"), both),
        check_vma=False,
    )
```

```python
import functools
import jax
import jax.numpy as jnp
from jax import lax
from jax.experimental import pallas as pl
from jax.experimental.pallas import tpu as pltpu
from jax.sharding import PartitionSpec as P

HEADS = 8
HD = 64
TOK = 512
D = 512
EPS = 1e-6
F32 = jnp.float32
BF16 = jnp.bfloat16
JB = 128
OUT_OF_MASK = -1e30


def dot_nn(a, b):
    return lax.dot_general(a, b, (((1,), (0,)), ((), ())), preferred_element_type=F32)


def dot_nt(a, b):
    return lax.dot_general(a, b, (((1,), (1,)), ((), ())), preferred_element_type=F32)


def window(jb):
    lo = jb * JB
    return lo, min(TOK, -(-(lo + JB + 255) // 128) * 128)


def build_bias(len_ref, bias_ref):
    ends, total = [], 0
    for n in range(8):
        total = total + len_ref[0, n]
        ends.append(total)
    col = lax.broadcasted_iota(jnp.int32, (TOK, 1), 0)
    row = lax.broadcasted_iota(jnp.int32, (1, TOK), 1)
    seg_col = jnp.zeros((TOK, 1), jnp.int32)
    seg_row = jnp.zeros((1, TOK), jnp.int32)
    for n in range(8):
        seg_col = seg_col + (col >= ends[n]).astype(jnp.int32)
        seg_row = seg_row + (row >= ends[n]).astype(jnp.int32)
    for jb in range(TOK // JB):
        lo, hi = window(jb)
        keep = (seg_col[lo:lo + JB] == seg_row[:, lo:hi]) & (col[lo:lo + JB] <= row[:, lo:hi])
        bias_ref[lo:lo + JB, lo:hi] = jnp.where(keep, 0.0, OUT_OF_MASK)


def zero_corners(ref, lead):
    zeros = jnp.zeros(lead + (128, 128), ref.dtype)
    full = (slice(None),) * len(lead)
    ref[full + (slice(0, 128), slice(384, 512))] = zeros
    ref[full + (slice(128, 256), slice(0, 128))] = zeros
    ref[full + (slice(384, 512), slice(256, 384))] = zeros


def normalize_events(ev_ref, xnt_ref, normedt_ref, inv_ref):
    x = ev_ref[...].T.astype(F32)
    mean = jnp.mean(x, axis=0, keepdims=True)
    c = x - mean
    inv = lax.rsqrt(jnp.mean(c * c, axis=0, keepdims=True) + EPS)
    xn = c * inv
    xnt_ref[...] = xn
    normedt_ref[...] = xn.astype(BF16)
    inv_ref[...] = inv


def project(w_in_ref, normedt_ref, slope_ref, act_ref, half_ref):
    for c in range(16):
        lo = c * 128
        wt = w_in_ref[0:D, lo:lo + 128].T
        half = dot_nn(wt, normedt_ref[...]) * 0.5
        half_ref[lo:lo + 128, :] = half
        t = jnp.tanh(half)
        p = 1.0 + t
        act = half * p
        slope_ref[lo:lo + 128, :] = p + act * (1.0 - t)
        act_ref[lo:lo + 128, :] = act.astype(BF16)


def natural(act_ref, nat_ref):
    nat_ref[:, 0:512] = act_ref[512:1024, :].T
    nat_ref[:, 512:1024] = act_ref[1536:2048, :].T


def head_pair_cols(nat_ref, base, pair):
    return nat_ref[:, pl.ds(pl.multiple_of(base + pair * 128, 128), 128)]


def attend_head(h, act_ref, bias_ref, w_ref, dsl_ref, att_ref):
    r = pl.multiple_of(h * HD, HD)
    qt = act_ref[pl.ds(1024 + r, HD), :] * 0.0625
    kt = act_ref[pl.ds(1536 + r, HD), :]
    vt = act_ref[pl.ds(512 + r, HD), :] * (1.0 / 64.0)
    k = kt.T
    for jb in range(TOK // JB):
        lo, hi = window(jb)
        half = dot_nn(k[lo:lo + JB], qt[:, lo:hi]) + bias_ref[lo:lo + JB, lo:hi]
        t = jnp.tanh(half)
        p = 1.0 + t
        w = half * p
        w_ref[h, lo:lo + JB, lo:hi] = w.astype(BF16)
        dsl_ref[h, lo:lo + JB, lo:hi] = p + w * (1.0 - t)
    att_ref[pl.ds(r, HD), 0:256] = dot_nn(vt[:, 0:256], w_ref[h, 0:256, 0:256])
    att_ref[pl.ds(r, HD), 256:512] = dot_nn(vt, w_ref[h, :, 256:512])


def norm_att(att_ref, ainv_ref, act_ref, gated_ref):
    a = att_ref[...]
    mean = jnp.mean(a, axis=0, keepdims=True)
    c = a - mean
    inv = lax.rsqrt(jnp.mean(c * c, axis=0, keepdims=True) + EPS)
    an = c * inv
    att_ref[...] = an
    ainv_ref[...] = inv
    gated_ref[...] = (an * act_ref[0:512, :].astype(F32)).astype(BF16)


def put_z_grad(at, lanes, joined, slope_ref, half_ref, zg_ref, dot_ref):
    grad = (joined * slope_ref[at, lanes]).astype(BF16)
    zg_ref[at, lanes] = grad
    dot_ref[:, lanes] += jnp.sum(grad.astype(F32) * half_ref[at, lanes], axis=0, keepdims=True)


def att_backward(w_out_ref, up_ref, upt_ref, att_ref, ainv_ref, act_ref, ag_ref, z_refs):
    upt_ref[...] = up_ref[...].T
    gg = dot_nn(w_out_ref[...], upt_ref[...])
    an = att_ref[...]
    put_z_grad(slice(0, 512), slice(0, 512), gg * an, *z_refs)
    g = gg * act_ref[0:512, :].astype(F32)
    first = jnp.mean(g, axis=0, keepdims=True)
    second = jnp.mean(g * an, axis=0, keepdims=True)
    ag_ref[...] = ((g - first - an * second) * (ainv_ref[...] * (1.0 / 128.0))).astype(BF16)


def backward_head(h, act_ref, ag_ref, w_ref, dsl_ref, ds_ref, z_refs):
    r = h * HD
    qt = act_ref[1024 + r:1024 + r + HD, :]
    kt = act_ref[1536 + r:1536 + r + HD, :]
    v = act_ref[512 + r:512 + r + HD, :].T
    ag = ag_ref[r:r + HD, :]
    for jb in range(TOK // JB):
        lo, hi = window(jb)
        wg = dot_nn(v[lo:lo + JB], ag[:, lo:hi])
        ds_ref[lo:lo + JB, lo:hi] = (wg * dsl_ref[h, lo:lo + JB, lo:hi]).astype(BF16)
    left, right = slice(0, 256), slice(256, 512)
    rows = [slice(base + r, base + r + HD) for base in (512, 1024, 1536)]
    put_z_grad(rows[0], left, dot_nt(ag, w_ref[h, 0:256, :]) * 2.0, *z_refs)
    put_z_grad(rows[0], right, dot_nt(ag[:, right], w_ref[h, right, right]) * 2.0, *z_refs)
    put_z_grad(rows[1], left, dot_nn(kt[:, left], ds_ref[left, left]) * 0.125, *z_refs)
    put_z_grad(rows[1], right, dot_nn(kt, ds_ref[:, right]) * 0.125, *z_refs)
    put_z_grad(rows[2], left, dot_nt(qt, ds_ref[left, :]) * 0.125, *z_refs)
    put_z_grad(rows[2], right, dot_nt(qt[:, right], ds_ref[right, right]) * 0.125, *z_refs)


def sum_rows(w_in_ref):
    sums = dot_nn(jnp.ones((8, D), BF16), w_in_ref[0:D, :])
    high = sums.astype(BF16)
    w_in_ref[D:D + 16, :] = jnp.concatenate([high, (sums - high.astype(F32)).astype(BF16)], axis=0)


def event_gradient(path, w_in_ref, zg_ref, dot_ref, stat_ref, upt_ref, xnt_ref, inv_ref):
    if path == 0:
        ng = dot_nn(w_in_ref[256:D + 16, :], zg_ref[...])
        stat_ref[0:1, :] = (ng[256:257] + ng[264:265]) * (1.0 / 512.0)
        stat_ref[1:2, :] = dot_ref[...] * (1.0 / 256.0)
        ng = ng[0:256]
        at = slice(256, 512)
    else:
        at = slice(0, 256)
        ng = dot_nn(w_in_ref[at, :], zg_ref[...])
    back = (ng - stat_ref[0:1, :] - xnt_ref[at, :] * stat_ref[1:2, :]) * (inv_ref[...] * 0.5)
    return (upt_ref[at, :].astype(F32) + back).astype(BF16)


MESH = pl.DeviceIdType.MESH
SLOTS = 1024
ROWS_DEV = 1024
PLACE_BLOCKS = 4


def log2(n):
    return n.bit_length() - 1


def one_hot(rows, cols_of):
    at = lax.broadcasted_iota(jnp.int32, (rows, cols_of.shape[1]), 0)
    return jnp.where(at == cols_of, 1.0, 0.0).astype(BF16)


def start_all(axis, size, rows, src_ref, dst_ref, send_sem, recv_sem, lo=0, step=1):
    at = lax.axis_index(axis)
    me = lax.div(at - lo, step)
    mine = pl.ds(pl.multiple_of(me * rows, rows), rows)
    pltpu.make_async_copy(src_ref.at[mine], dst_ref.at[mine], recv_sem).start()

    def send(k, carry):
        peer = lax.rem(me + k, size)
        pltpu.make_async_remote_copy(
            src_ref=src_ref.at[pl.ds(pl.multiple_of(peer * rows, rows), rows)],
            dst_ref=dst_ref.at[mine],
            send_sem=send_sem,
            recv_sem=recv_sem,
            device_id={axis: lo + peer * step},
            device_id_type=MESH,
        ).start()
        return carry

    lax.fori_loop(1, size, send, 0)


def wait_bytes(ref, sem):
    pltpu.make_async_copy(ref, ref, sem).wait()


def route_slots(owner_ref, item_ref, n_dp, n_table, oh_a, oh_b, meta_ref):
    pairs = n_dp * n_table
    cap = SLOTS // pairs
    row = owner_ref[...]
    col = jnp.broadcast_to(row, (128, TOK)).T[:, 0:1]
    place_col = lax.broadcasted_iota(jnp.int32, (TOK, 1), 0)
    place_row = lax.broadcasted_iota(jnp.int32, (1, TOK), 1)
    earlier = (col == row) & (place_col < place_row)
    rank = jnp.sum(jnp.where(earlier, 1.0, 0.0), axis=0, keepdims=True).astype(jnp.int32)
    table, dp = row & (n_table - 1), row >> log2(n_table)
    oh_a[...] = one_hot(SLOTS, table * (n_dp * cap) + dp * cap + rank)
    oh_b[...] = one_hot(SLOTS, dp * (n_table * cap) + table * cap + rank)
    code = item_ref[...] + 1
    line = lax.broadcasted_iota(jnp.int32, (128, TOK), 0)
    words = jnp.where((line & 1) == 0, code >> 5, code & 31).astype(F32)
    meta_t = jnp.where((line >> 1) == rank, words, 0.0).astype(BF16)
    meta_ref[...] = dot_nt(one_hot(pairs, table * n_dp + dp), meta_t).astype(BF16)


def swap_rows(first, second, cap):
    n = first * second * cap
    out = lax.broadcasted_iota(jnp.int32, (n, 1), 0)
    slot = out & (cap - 1)
    a = (out >> log2(cap)) & (first - 1)
    b = out >> (log2(cap) + log2(first))
    at = lax.broadcasted_iota(jnp.int32, (n, n), 1)
    return jnp.where(at == a * (second * cap) + b * cap + slot, 1.0, 0.0).astype(BF16)


def item_lanes(meta, n_dp, n_table):
    pairs = n_dp * n_table
    cap = SLOTS // pairs
    lines = meta.astype(F32).T.astype(BF16)
    col = lax.broadcasted_iota(jnp.int32, (1, SLOTS), 1)
    word = lax.broadcasted_iota(jnp.int32, (128, SLOTS), 0)
    slot, pair = col & (cap - 1), col >> log2(cap)
    other = (pair & (n_dp - 1)) * n_table + (pair >> log2(n_dp))
    items = []
    for order in (pair, other):
        spread = dot_nn(lines, one_hot(pairs, order))
        high = jnp.sum(jnp.where(word == 2 * slot, spread, 0.0), axis=0, keepdims=True)
        low = jnp.sum(jnp.where(word == 2 * slot + 1, spread, 0.0), axis=0, keepdims=True)
        items.append((high * 32.0 + low - 1.0).astype(jnp.int32))
    return items


def kernel(n_dp, n_table, *refs):
    names = INPUTS + OUTPUTS + tuple(scratch(n_dp, n_table))
    ns = type("Refs", (), dict(zip(names, refs)))
    dp, table = lax.axis_index("dp"), lax.axis_index("table")
    core = lax.rem(dp, 2)
    pairs = n_dp * n_table
    cap = SLOTS // pairs
    nx = 4
    ny = n_table // nx
    row_share, col_share, half_dp = D // n_table, D // n_dp, n_dp // 2
    x_rows = ny * row_share

    barrier = pltpu.get_barrier_semaphore()
    for axis, size, me in (("table", n_table, table), ("dp", n_dp, dp)):
        def greet(k, carry, axis=axis, size=size, me=me):
            pl.semaphore_signal(
                barrier, inc=1, device_id={axis: lax.rem(me + k, size)}, device_id_type=MESH
            )
            return carry
        lax.fori_loop(1, size, greet, 0)

    loads = {}
    for n, name in enumerate(("events", "w_in", "w_out", "upstream")):
        held = getattr(ns, name + "_v")
        held = held.at[pl.ds(0, D)] if name == "w_in" else held
        loads[name] = pltpu.make_async_copy(getattr(ns, name), held, ns.load.at[n])
        loads[name].start()

    route_slots(ns.owners, ns.items, n_dp, n_table, ns.oh_a, ns.oh_b, ns.meta.at[0])
    build_bias(ns.lengths, ns.bias)
    zero_corners(ns.w, (HEADS,))
    zero_corners(ns.ds, ())
    loads["events"].wait()
    normalize_events(ns.events_v, ns.xnt, ns.normedt, ns.inv)
    loads["w_in"].wait()
    project(ns.w_in_v, ns.normedt, ns.slope, ns.act, ns.half)
    sum_rows(ns.w_in_v)

    for h in range(HEADS):
        attend_head(h, ns.act, ns.bias, ns.w, ns.dsl, ns.att)
    norm_att(ns.att, ns.ainv, ns.act, ns.gated)
    loads["upstream"].wait()
    for half in range(2):
        ns.part[half] = dot_nn(ns.gated[...], ns.upstream_v[:, half * 256:half * 256 + 256])
    pl.semaphore_wait(barrier, n_table + n_dp - 2)
    start_all("table", n_table, n_dp, ns.meta.at[0], ns.meta.at[1], ns.send.at[0], ns.recv.at[0])
    to_core = pltpu.make_async_remote_copy(
        src_ref=ns.part.at[1 - core],
        dst_ref=ns.other,
        send_sem=ns.send.at[2],
        recv_sem=ns.recv.at[2],
        device_id={"dp": dp + 1 - 2 * core},
        device_id_type=MESH,
    )
    to_core.start()
    loads["w_out"].wait()
    ns.dot[...] = jnp.zeros_like(ns.dot)
    z_refs = (ns.slope, ns.half, ns.zg, ns.dot)
    att_backward(ns.w_out_v, ns.upstream_v, ns.upt, ns.att, ns.ainv, ns.act, ns.ag, z_refs)
    for h in range(HEADS):
        backward_head(h, ns.act, ns.ag, ns.w, ns.dsl, ns.ds, z_refs)

    first = (("table", n_table, n_dp * cap), ("dp", n_dp, n_table * cap))
    second = first[::-1]

    def hop_one(path, half):
        lanes = pl.ds(half * 128, 128)
        start_all(
            *first[path], ns.moved.at[path, :, lanes], ns.landed.at[path, half],
            ns.hop_send.at[path, half, 0], ns.hop_recv.at[path, half, 0],
        )

    def hop_two(path, half):
        swap = (ns.swap_a, ns.swap_b)[path]
        wait_bytes(ns.landed.at[path, half], ns.hop_recv.at[path, half, 0])
        ns.again[path, half] = dot_nn(swap[...], ns.landed[path, half]).astype(BF16)
        start_all(
            *second[path], ns.again.at[path, half], ns.arrived.at[path, :, pl.ds(half * 128, 128)],
            ns.hop_send.at[path, half, 1], ns.hop_recv.at[path, half, 1],
        )

    for path, slots in ((0, ns.oh_a), (1, ns.oh_b)):
        grad = event_gradient(path, ns.w_in_v, ns.zg, ns.dot, ns.stat, ns.upt, ns.xnt, ns.inv)
        ns.moved[path] = dot_nt(slots[...], grad).astype(BF16)
        hop_one(path, 0)
    hop_one(0, 1)
    hop_one(1, 1)

    to_core.wait_recv()
    for t in range(n_table):
        y, x = t // nx, t % nx
        rows = slice(t * row_share, (t + 1) * row_share)
        ns.x_send[x * x_rows + y * row_share:x * x_rows + (y + 1) * row_share] = (
            ns.part[core, rows] + ns.other[rows]
        ).astype(BF16)
    start_all("table", nx, x_rows, ns.x_send, ns.x_recv, ns.send.at[3], ns.recv.at[3], lo=lax.div(table, nx) * nx)
    wait_bytes(ns.meta.at[1], ns.recv.at[0])
    ns.meta[2] = dot_nn(swap_rows(n_table, n_dp, 1), ns.meta[1]).astype(BF16)
    start_all("dp", n_dp, n_table, ns.meta.at[2], ns.meta.at[3], ns.send.at[1], ns.recv.at[1])
    ns.swap_a[...] = swap_rows(n_table, n_dp, cap)
    ns.swap_b[...] = swap_rows(n_dp, n_table, cap)

    wait_bytes(ns.x_recv, ns.recv.at[3])
    share = ns.x_recv[0:x_rows].astype(F32)
    for x in range(1, nx):
        share = share + ns.x_recv[x * x_rows:(x + 1) * x_rows].astype(F32)
    ns.y_send[...] = share.astype(BF16)
    start_all("table", ny, row_share, ns.y_send, ns.y_recv, ns.send.at[4], ns.recv.at[4], lo=lax.rem(table, nx), step=nx)

    hop_two(0, 0)
    hop_two(1, 0)

    wait_bytes(ns.y_recv, ns.recv.at[4])
    share = ns.y_recv[0:row_share].astype(F32)
    for y in range(1, ny):
        share = share + ns.y_recv[y * row_share:(y + 1) * row_share].astype(F32)
    for g in range(2):
        ns.fin_send[g] = share[:, g * 128:g * 128 + 128]
    z = lax.div(dp, 2)
    for m in range(half_dp):
        target = core * half_dp + m
        group = ns.fin_send.at[m * col_share // 128]

        @pl.when(target == dp)
        def _():
            pltpu.make_async_copy(group, ns.fin_recv.at[z], ns.recv.at[5]).start()

        @pl.when(target != dp)
        def _():
            pltpu.make_async_remote_copy(
                src_ref=group,
                dst_ref=ns.fin_recv.at[z],
                send_sem=ns.fin_sem.at[m],
                recv_sem=ns.recv.at[5],
                device_id={"dp": target},
                device_id_type=MESH,
            ).start()

    wait_bytes(ns.meta.at[3], ns.recv.at[1])
    items = item_lanes(ns.meta[3], n_dp, n_table)
    ns.item_rows[0:1, :] = items[0]
    ns.item_rows[1:2, :] = items[1]

    hop_two(0, 1)
    hop_two(1, 1)

    wait_bytes(ns.fin_recv, ns.recv.at[5])
    total = ns.fin_recv[0]
    for k in range(1, half_dp):
        total = total + ns.fin_recv[k]
    lane = lax.rem(lax.rem(dp, half_dp) * col_share, 128)
    block = total[:, 0:col_share]
    for at in range(col_share, 128, col_share):
        block = jnp.where(lane == at, total[:, at:at + col_share], block)
    ns.grad_block[...] = block

    wait_bytes(ns.meta.at[0, pl.ds(0, (n_table - 1) * n_dp)], ns.send.at[0])
    wait_bytes(ns.meta.at[2, pl.ds(0, (n_dp - 1) * n_table)], ns.send.at[1])
    to_core.wait_send()
    wait_bytes(ns.x_send.at[pl.ds(0, (nx - 1) * x_rows)], ns.send.at[3])
    if ny > 1:
        wait_bytes(ns.y_send.at[pl.ds(0, (ny - 1) * row_share)], ns.send.at[4])
    for m in range(half_dp):
        target = core * half_dp + m

        @pl.when(target != dp)
        def _():
            wait_bytes(ns.fin_send.at[m * col_share // 128], ns.fin_sem.at[m])
    for half in range(2):
        for path in range(2):
            for hop, (_, size, rows) in enumerate((first[path], second[path])):
                wait_bytes(ns.again.at[path, half, pl.ds(0, (size - 1) * rows)], ns.hop_send.at[path, half, hop])
    for half in range(2):
        for path in range(2):
            wait_bytes(ns.arrived.at[path, :, pl.ds(half * 128, 128)], ns.hop_recv.at[path, half, 1])


def place_kernel(arrived_ref, item_ref, block_ref, out_ref, table_ref, rows, built, load, store):
    copies = [pltpu.make_async_copy(arrived_ref.at[p], rows.at[p], load.at[p]) for p in range(2)]
    for copy in copies:
        copy.start()
    out_ref[...] = block_ref[...]
    blocks = built.shape[0]
    size = ROWS_DEV // blocks
    stores = []
    for b in range(blocks):
        for p in range(2):
            hits = one_hot(size, item_ref[p:p + 1, :] - b * size)
            if b == 0:
                copies[p].wait()
            built[b, :, 256 - p * 256:512 - p * 256] = dot_nn(hits, rows[p]).astype(BF16)
        stores.append(pltpu.make_async_copy(built.at[b], table_ref.at[pl.ds(b * size, size)], store.at[b]))
        stores[-1].start()
    for copy in stores:
        copy.wait()


INPUTS = ("events", "upstream", "w_in", "w_out", "lengths", "owners", "items")
OUTPUTS = ("grad_block", "item_rows", "arrived")


def scratch(n_dp, n_table):
    row_share = D // n_table
    pairs = n_dp * n_table
    vmem = pltpu.VMEM
    dma = pltpu.SemaphoreType.DMA
    return dict(
        events_v=vmem((TOK, D), BF16),
        upstream_v=vmem((TOK, D), BF16),
        w_in_v=vmem((D + 16, 4 * D), BF16),
        half=vmem((4 * D, TOK), F32),
        upt=vmem((D, TOK), BF16),
        dot=vmem((1, TOK), F32),
        stat=vmem((8, TOK), F32),
        w_out_v=vmem((D, D), BF16),
        bias=vmem((TOK, TOK), F32),
        xnt=vmem((D, TOK), F32),
        normedt=vmem((D, TOK), BF16),
        inv=vmem((1, TOK), F32),
        slope=vmem((4 * D, TOK), F32),
        act=vmem((4 * D, TOK), BF16),
        w=vmem((HEADS, TOK, TOK), BF16),
        dsl=vmem((HEADS, TOK, TOK), F32),
        att=vmem((D, TOK), F32),
        ainv=vmem((1, TOK), F32),
        gated=vmem((D, TOK), BF16),
        zg=vmem((4 * D, TOK), BF16),
        ag=vmem((D, TOK), BF16),
        ds=vmem((TOK, TOK), BF16),
        oh_a=vmem((SLOTS, TOK), BF16),
        oh_b=vmem((SLOTS, TOK), BF16),
        swap_a=vmem((SLOTS, SLOTS), BF16),
        swap_b=vmem((SLOTS, SLOTS), BF16),
        meta=vmem((4, pairs, 128), BF16),
        moved=vmem((2, SLOTS, 256), BF16),
        landed=vmem((2, 2, SLOTS, 128), BF16),
        again=vmem((2, 2, SLOTS, 128), BF16),
        part=vmem((2, D, 256), F32),
        other=vmem((D, 256), F32),
        x_send=vmem((D, 256), BF16),
        x_recv=vmem((D, 256), BF16),
        y_send=vmem((D // 4, 256), BF16),
        y_recv=vmem((D // 4, 256), BF16),
        fin_send=vmem((2, row_share, 128), F32),
        fin_recv=vmem((n_dp // 2, row_share, 128), F32),
        load=dma((4,)),
        send=dma((6,)),
        recv=dma((6,)),
        hop_send=dma((2, 2, 2)),
        hop_recv=dma((2, 2, 2)),
        fin_sem=dma((n_dp // 2,)),
    )


def solution(mesh):
    n_dp, n_table = mesh.shape["dp"], mesh.shape["table"]
    in_vmem = pl.BlockSpec(memory_space=pltpu.VMEM)
    in_smem = pl.BlockSpec(memory_space=pltpu.SMEM)
    anywhere = pl.BlockSpec(memory_space=pl.ANY)

    def local(events, upstream, w_in, w_out, lengths, owners, item_rows):
        block = jax.ShapeDtypeStruct((D // n_table, D // n_dp), F32)
        grad_block, items, arrived = pl.pallas_call(
            functools.partial(kernel, n_dp, n_table),
            out_shape=(
                block,
                jax.ShapeDtypeStruct((8, SLOTS), jnp.int32),
                jax.ShapeDtypeStruct((2, SLOTS, 256), BF16),
            ),
            in_specs=[anywhere] * 4 + [in_smem] + [in_vmem] * 2,
            out_specs=(in_vmem, in_vmem, anywhere),
            scratch_shapes=list(scratch(n_dp, n_table).values()),
            compiler_params=pltpu.CompilerParams(
                collective_id=0, has_side_effects=True, vmem_limit_bytes=60 << 20
            ),
        )(events, upstream, w_in, w_out, lengths, owners.reshape(1, TOK), item_rows.reshape(1, TOK))
        return pl.pallas_call(
            place_kernel,
            out_shape=(block, jax.ShapeDtypeStruct((ROWS_DEV, D), BF16)),
            in_specs=[anywhere, in_vmem, in_vmem],
            out_specs=(in_vmem, anywhere),
            scratch_shapes=[
                pltpu.VMEM((2, SLOTS, 256), BF16),
                pltpu.VMEM((PLACE_BLOCKS, ROWS_DEV // PLACE_BLOCKS, D), BF16),
                pltpu.SemaphoreType.DMA((2,)),
                pltpu.SemaphoreType.DMA((PLACE_BLOCKS,)),
            ],
            compiler_params=pltpu.CompilerParams(vmem_limit_bytes=60 << 20),
        )(arrived, items, grad_block)

    both = P(("dp", "table"), None)
    return jax.shard_map(
        local,
        mesh=mesh,
        in_specs=(both, both, P(), P(), both, both, P(("dp", "table"))),
        out_specs=(P("table", "dp"), both),
        check_vma=False,
    )
```

```python
import functools
import jax
import jax.numpy as jnp
from jax import lax
from jax.experimental import pallas as pl
from jax.experimental.pallas import tpu as pltpu
from jax.sharding import PartitionSpec as P

HEADS = 8
HD = 64
TOK = 512
D = 512
EPS = 1e-6
F32 = jnp.float32
BF16 = jnp.bfloat16
JB = 128
OUT_OF_MASK = -1e30


def dot_nn(a, b):
    return lax.dot_general(a, b, (((1,), (0,)), ((), ())), preferred_element_type=F32)


def dot_nt(a, b):
    return lax.dot_general(a, b, (((1,), (1,)), ((), ())), preferred_element_type=F32)


def window(jb):
    lo = jb * JB
    return lo, min(TOK, -(-(lo + JB + 255) // 128) * 128)


def build_bias(len_ref, bias_ref):
    ends, total = [], 0
    for n in range(8):
        total = total + len_ref[0, n]
        ends.append(total)
    col = lax.broadcasted_iota(jnp.int32, (TOK, 1), 0)
    row = lax.broadcasted_iota(jnp.int32, (1, TOK), 1)
    seg_col = jnp.zeros((TOK, 1), jnp.int32)
    seg_row = jnp.zeros((1, TOK), jnp.int32)
    for n in range(8):
        seg_col = seg_col + (col >= ends[n]).astype(jnp.int32)
        seg_row = seg_row + (row >= ends[n]).astype(jnp.int32)
    for jb in range(TOK // JB):
        lo, hi = window(jb)
        keep = (seg_col[lo:lo + JB] == seg_row[:, lo:hi]) & (col[lo:lo + JB] <= row[:, lo:hi])
        bias_ref[lo:lo + JB, lo:hi] = jnp.where(keep, 0.0, OUT_OF_MASK)


def zero_corners(ref, lead):
    zeros = jnp.zeros(lead + (128, 128), ref.dtype)
    full = (slice(None),) * len(lead)
    ref[full + (slice(0, 128), slice(384, 512))] = zeros
    ref[full + (slice(128, 256), slice(0, 128))] = zeros
    ref[full + (slice(384, 512), slice(256, 384))] = zeros


def normalize_events(ev_ref, xnt_ref, normedt_ref, inv_ref):
    x = ev_ref[...].T.astype(F32)
    mean = jnp.mean(x, axis=0, keepdims=True)
    c = x - mean
    inv = lax.rsqrt(jnp.mean(c * c, axis=0, keepdims=True) + EPS)
    xn = c * inv
    xnt_ref[...] = xn
    normedt_ref[...] = xn.astype(BF16)
    inv_ref[...] = inv


def project(w_in_ref, normedt_ref, slope_ref, act_ref, half_ref):
    for c in range(16):
        lo = c * 128
        wt = w_in_ref[0:D, lo:lo + 128].T
        half = dot_nn(wt, normedt_ref[...]) * 0.5
        half_ref[lo:lo + 128, :] = half
        t = jnp.tanh(half)
        p = 1.0 + t
        act = half * p
        slope_ref[lo:lo + 128, :] = p + act * (1.0 - t)
        act_ref[lo:lo + 128, :] = act.astype(BF16)


def natural(act_ref, nat_ref):
    nat_ref[:, 0:512] = act_ref[512:1024, :].T
    nat_ref[:, 512:1024] = act_ref[1536:2048, :].T


def head_pair_cols(nat_ref, base, pair):
    return nat_ref[:, pl.ds(pl.multiple_of(base + pair * 128, 128), 128)]


def attend_head(h, act_ref, bias_ref, w_ref, dsl_ref, att_ref):
    r = pl.multiple_of(h * HD, HD)
    qt = act_ref[pl.ds(1024 + r, HD), :] * 0.0625
    kt = act_ref[pl.ds(1536 + r, HD), :]
    vt = act_ref[pl.ds(512 + r, HD), :] * (1.0 / 64.0)
    k = kt.T
    for jb in range(TOK // JB):
        lo, hi = window(jb)
        half = dot_nn(k[lo:lo + JB], qt[:, lo:hi]) + bias_ref[lo:lo + JB, lo:hi]
        t = jnp.tanh(half)
        p = 1.0 + t
        w = half * p
        w_ref[h, lo:lo + JB, lo:hi] = w.astype(BF16)
        dsl_ref[h, lo:lo + JB, lo:hi] = p + w * (1.0 - t)
    att_ref[pl.ds(r, HD), 0:256] = dot_nn(vt[:, 0:256], w_ref[h, 0:256, 0:256])
    att_ref[pl.ds(r, HD), 256:512] = dot_nn(vt, w_ref[h, :, 256:512])


def norm_att(att_ref, ainv_ref, act_ref, gated_ref):
    a = att_ref[...]
    mean = jnp.mean(a, axis=0, keepdims=True)
    c = a - mean
    inv = lax.rsqrt(jnp.mean(c * c, axis=0, keepdims=True) + EPS)
    an = c * inv
    att_ref[...] = an
    ainv_ref[...] = inv
    gated_ref[...] = (an * act_ref[0:512, :].astype(F32)).astype(BF16)


def put_z_grad(at, lanes, joined, slope_ref, half_ref, zg_ref, dot_ref):
    grad = (joined * slope_ref[at, lanes]).astype(BF16)
    zg_ref[at, lanes] = grad
    dot_ref[:, lanes] += jnp.sum(grad.astype(F32) * half_ref[at, lanes], axis=0, keepdims=True)


def att_backward(w_out_ref, up_ref, upt_ref, att_ref, ainv_ref, act_ref, ag_ref, z_refs):
    upt_ref[...] = up_ref[...].T
    gg = dot_nn(w_out_ref[...], upt_ref[...])
    an = att_ref[...]
    put_z_grad(slice(0, 512), slice(0, 512), gg * an, *z_refs)
    g = gg * act_ref[0:512, :].astype(F32)
    first = jnp.mean(g, axis=0, keepdims=True)
    second = jnp.mean(g * an, axis=0, keepdims=True)
    ag_ref[...] = ((g - first - an * second) * (ainv_ref[...] * (1.0 / 128.0))).astype(BF16)


def backward_head(h, act_ref, ag_ref, w_ref, dsl_ref, ds_ref, z_refs):
    r = h * HD
    qt = act_ref[1024 + r:1024 + r + HD, :]
    kt = act_ref[1536 + r:1536 + r + HD, :]
    v = act_ref[512 + r:512 + r + HD, :].T
    ag = ag_ref[r:r + HD, :]
    for jb in range(TOK // JB):
        lo, hi = window(jb)
        wg = dot_nn(v[lo:lo + JB], ag[:, lo:hi])
        ds_ref[lo:lo + JB, lo:hi] = (wg * dsl_ref[h, lo:lo + JB, lo:hi]).astype(BF16)
    left, right = slice(0, 256), slice(256, 512)
    rows = [slice(base + r, base + r + HD) for base in (512, 1024, 1536)]
    put_z_grad(rows[0], left, dot_nt(ag, w_ref[h, 0:256, :]) * 2.0, *z_refs)
    put_z_grad(rows[0], right, dot_nt(ag[:, right], w_ref[h, right, right]) * 2.0, *z_refs)
    put_z_grad(rows[1], left, dot_nn(kt[:, left], ds_ref[left, left]) * 0.125, *z_refs)
    put_z_grad(rows[1], right, dot_nn(kt, ds_ref[:, right]) * 0.125, *z_refs)
    put_z_grad(rows[2], left, dot_nt(qt, ds_ref[left, :]) * 0.125, *z_refs)
    put_z_grad(rows[2], right, dot_nt(qt[:, right], ds_ref[right, right]) * 0.125, *z_refs)


def sum_rows(w_in_ref):
    sums = dot_nn(jnp.ones((8, D), BF16), w_in_ref[0:D, :])
    high = sums.astype(BF16)
    w_in_ref[D:D + 16, :] = jnp.concatenate([high, (sums - high.astype(F32)).astype(BF16)], axis=0)


def event_gradient(path, w_in_ref, zg_ref, dot_ref, stat_ref, upt_ref, xnt_ref, inv_ref):
    if path == 0:
        ng = dot_nn(w_in_ref[256:D + 16, :], zg_ref[...])
        stat_ref[0:1, :] = (ng[256:257] + ng[264:265]) * (1.0 / 512.0)
        stat_ref[1:2, :] = dot_ref[...] * (1.0 / 256.0)
        ng = ng[0:256]
        at = slice(256, 512)
    else:
        at = slice(0, 256)
        ng = dot_nn(w_in_ref[at, :], zg_ref[...])
    back = (ng - stat_ref[0:1, :] - xnt_ref[at, :] * stat_ref[1:2, :]) * (inv_ref[...] * 0.5)
    return (upt_ref[at, :].astype(F32) + back).astype(BF16)


MESH = pl.DeviceIdType.MESH
SLOTS = 1024
ROWS_DEV = 1024
PLACE_BLOCKS = 4


def log2(n):
    return n.bit_length() - 1


def one_hot(rows, cols_of):
    at = lax.broadcasted_iota(jnp.int32, (rows, cols_of.shape[1]), 0)
    return jnp.where(at == cols_of, 1.0, 0.0).astype(BF16)


def start_all(axis, size, rows, src_ref, dst_ref, send_sem, recv_sem, lo=0, step=1):
    at = lax.axis_index(axis)
    me = lax.div(at - lo, step)
    mine = pl.ds(pl.multiple_of(me * rows, rows), rows)
    pltpu.make_async_copy(src_ref.at[mine], dst_ref.at[mine], recv_sem).start()

    def send(k, carry):
        peer = lax.rem(me + k, size)
        pltpu.make_async_remote_copy(
            src_ref=src_ref.at[pl.ds(pl.multiple_of(peer * rows, rows), rows)],
            dst_ref=dst_ref.at[mine],
            send_sem=send_sem,
            recv_sem=recv_sem,
            device_id={axis: lo + peer * step},
            device_id_type=MESH,
        ).start()
        return carry

    lax.fori_loop(1, size, send, 0)


def wait_bytes(ref, sem):
    pltpu.make_async_copy(ref, ref, sem).wait()


def route_slots(owner_ref, item_ref, n_dp, n_table, oh_a, oh_b, meta_ref):
    pairs = n_dp * n_table
    cap = SLOTS // pairs
    row = owner_ref[...]
    col = jnp.broadcast_to(row, (128, TOK)).T[:, 0:1]
    place_col = lax.broadcasted_iota(jnp.int32, (TOK, 1), 0)
    place_row = lax.broadcasted_iota(jnp.int32, (1, TOK), 1)
    earlier = (col == row) & (place_col < place_row)
    rank = jnp.sum(jnp.where(earlier, 1.0, 0.0), axis=0, keepdims=True).astype(jnp.int32)
    table, dp = row & (n_table - 1), row >> log2(n_table)
    oh_a[...] = one_hot(SLOTS, table * (n_dp * cap) + dp * cap + rank)
    oh_b[...] = one_hot(SLOTS, dp * (n_table * cap) + table * cap + rank)
    code = item_ref[...] + 1
    line = lax.broadcasted_iota(jnp.int32, (128, TOK), 0)
    words = jnp.where((line & 1) == 0, code >> 5, code & 31).astype(F32)
    meta_t = jnp.where((line >> 1) == rank, words, 0.0).astype(BF16)
    meta_ref[...] = dot_nt(one_hot(pairs, table * n_dp + dp), meta_t).astype(BF16)


def swap_rows(first, second, cap):
    n = first * second * cap
    out = lax.broadcasted_iota(jnp.int32, (n, 1), 0)
    slot = out & (cap - 1)
    a = (out >> log2(cap)) & (first - 1)
    b = out >> (log2(cap) + log2(first))
    at = lax.broadcasted_iota(jnp.int32, (n, n), 1)
    return jnp.where(at == a * (second * cap) + b * cap + slot, 1.0, 0.0).astype(BF16)


def item_lanes(meta, n_dp, n_table):
    pairs = n_dp * n_table
    cap = SLOTS // pairs
    lines = meta.astype(F32).T.astype(BF16)
    col = lax.broadcasted_iota(jnp.int32, (1, SLOTS), 1)
    word = lax.broadcasted_iota(jnp.int32, (128, SLOTS), 0)
    slot, pair = col & (cap - 1), col >> log2(cap)
    other = (pair & (n_dp - 1)) * n_table + (pair >> log2(n_dp))
    items = []
    for order in (pair, other):
        spread = dot_nn(lines, one_hot(pairs, order))
        high = jnp.sum(jnp.where(word == 2 * slot, spread, 0.0), axis=0, keepdims=True)
        low = jnp.sum(jnp.where(word == 2 * slot + 1, spread, 0.0), axis=0, keepdims=True)
        items.append((high * 32.0 + low - 1.0).astype(jnp.int32))
    return items


def kernel(n_dp, n_table, *refs):
    names = INPUTS + OUTPUTS + tuple(scratch(n_dp, n_table))
    ns = type("Refs", (), dict(zip(names, refs)))
    dp, table = lax.axis_index("dp"), lax.axis_index("table")
    core = lax.rem(dp, 2)
    pairs = n_dp * n_table
    cap = SLOTS // pairs
    nx = 4
    ny = n_table // nx
    row_share, col_share, half_dp = D // n_table, D // n_dp, n_dp // 2
    x_rows = ny * row_share

    barrier = pltpu.get_barrier_semaphore()
    for axis, size, me in (("table", n_table, table), ("dp", n_dp, dp)):
        def greet(k, carry, axis=axis, size=size, me=me):
            pl.semaphore_signal(
                barrier, inc=1, device_id={axis: lax.rem(me + k, size)}, device_id_type=MESH
            )
            return carry
        lax.fori_loop(1, size, greet, 0)

    loads = {}
    for n, name in enumerate(("events", "w_in", "w_out", "upstream")):
        held = getattr(ns, name + "_v")
        held = held.at[pl.ds(0, D)] if name == "w_in" else held
        loads[name] = pltpu.make_async_copy(getattr(ns, name), held, ns.load.at[n])
        loads[name].start()

    route_slots(ns.owners, ns.items, n_dp, n_table, ns.oh_a, ns.oh_b, ns.meta.at[0])
    build_bias(ns.lengths, ns.bias)
    zero_corners(ns.w, (HEADS,))
    zero_corners(ns.ds, ())
    loads["events"].wait()
    normalize_events(ns.events_v, ns.xnt, ns.normedt, ns.inv)
    loads["w_in"].wait()
    project(ns.w_in_v, ns.normedt, ns.slope, ns.act, ns.half)
    sum_rows(ns.w_in_v)

    for h in range(HEADS):
        attend_head(h, ns.act, ns.bias, ns.w, ns.dsl, ns.att)
    norm_att(ns.att, ns.ainv, ns.act, ns.gated)
    loads["upstream"].wait()
    for half in range(2):
        ns.part[half] = dot_nn(ns.gated[...], ns.upstream_v[:, half * 256:half * 256 + 256])
    pl.semaphore_wait(barrier, n_table + n_dp - 2)
    start_all("table", n_table, n_dp, ns.meta.at[0], ns.meta.at[1], ns.send.at[0], ns.recv.at[0])
    to_core = pltpu.make_async_remote_copy(
        src_ref=ns.part.at[1 - core],
        dst_ref=ns.other,
        send_sem=ns.send.at[2],
        recv_sem=ns.recv.at[2],
        device_id={"dp": dp + 1 - 2 * core},
        device_id_type=MESH,
    )
    to_core.start()
    loads["w_out"].wait()
    ns.dot[...] = jnp.zeros_like(ns.dot)
    z_refs = (ns.slope, ns.half, ns.zg, ns.dot)
    att_backward(ns.w_out_v, ns.upstream_v, ns.upt, ns.att, ns.ainv, ns.act, ns.ag, z_refs)
    for h in range(HEADS):
        backward_head(h, ns.act, ns.ag, ns.w, ns.dsl, ns.ds, z_refs)
        if h == 5:
            to_core.wait_recv()
            for t in range(n_table):
                y, x = t // nx, t % nx
                rows = slice(t * row_share, (t + 1) * row_share)
                ns.x_send[x * x_rows + y * row_share:x * x_rows + (y + 1) * row_share] = (
                    ns.part[core, rows] + ns.other[rows]
                ).astype(BF16)
            start_all("table", nx, x_rows, ns.x_send, ns.x_recv, ns.send.at[3], ns.recv.at[3], lo=lax.div(table, nx) * nx)

    first = (("table", n_table, n_dp * cap), ("dp", n_dp, n_table * cap))
    second = first[::-1]

    def hop_one(path, half):
        lanes = pl.ds(half * 128, 128)
        start_all(
            *first[path], ns.moved.at[path, :, lanes], ns.landed.at[path, half],
            ns.hop_send.at[path, half, 0], ns.hop_recv.at[path, half, 0],
        )

    def hop_two(path, half):
        swap = (ns.swap_a, ns.swap_b)[path]
        wait_bytes(ns.landed.at[path, half], ns.hop_recv.at[path, half, 0])
        ns.again[path, half] = dot_nn(swap[...], ns.landed[path, half]).astype(BF16)
        start_all(
            *second[path], ns.again.at[path, half], ns.arrived.at[path, :, pl.ds(half * 128, 128)],
            ns.hop_send.at[path, half, 1], ns.hop_recv.at[path, half, 1],
        )

    for path, slots in ((0, ns.oh_a), (1, ns.oh_b)):
        grad = event_gradient(path, ns.w_in_v, ns.zg, ns.dot, ns.stat, ns.upt, ns.xnt, ns.inv)
        ns.moved[path] = dot_nt(slots[...], grad).astype(BF16)
        hop_one(path, 0)
    hop_one(0, 1)
    hop_one(1, 1)

    wait_bytes(ns.meta.at[1], ns.recv.at[0])
    ns.meta[2] = dot_nn(swap_rows(n_table, n_dp, 1), ns.meta[1]).astype(BF16)
    start_all("dp", n_dp, n_table, ns.meta.at[2], ns.meta.at[3], ns.send.at[1], ns.recv.at[1])
    ns.swap_a[...] = swap_rows(n_table, n_dp, cap)
    ns.swap_b[...] = swap_rows(n_dp, n_table, cap)

    wait_bytes(ns.x_recv, ns.recv.at[3])
    share = ns.x_recv[0:x_rows].astype(F32)
    for x in range(1, nx):
        share = share + ns.x_recv[x * x_rows:(x + 1) * x_rows].astype(F32)
    ns.y_send[...] = share.astype(BF16)
    start_all("table", ny, row_share, ns.y_send, ns.y_recv, ns.send.at[4], ns.recv.at[4], lo=lax.rem(table, nx), step=nx)

    hop_two(0, 0)
    hop_two(1, 0)

    hop_two(0, 1)
    hop_two(1, 1)

    wait_bytes(ns.y_recv, ns.recv.at[4])
    share = ns.y_recv[0:row_share].astype(F32)
    for y in range(1, ny):
        share = share + ns.y_recv[y * row_share:(y + 1) * row_share].astype(F32)
    for g in range(2):
        ns.fin_send[g] = share[:, g * 128:g * 128 + 128]
    z = lax.div(dp, 2)
    for m in range(half_dp):
        target = core * half_dp + m
        group = ns.fin_send.at[m * col_share // 128]

        @pl.when(target == dp)
        def _():
            pltpu.make_async_copy(group, ns.fin_recv.at[z], ns.recv.at[5]).start()

        @pl.when(target != dp)
        def _():
            pltpu.make_async_remote_copy(
                src_ref=group,
                dst_ref=ns.fin_recv.at[z],
                send_sem=ns.fin_sem.at[m],
                recv_sem=ns.recv.at[5],
                device_id={"dp": target},
                device_id_type=MESH,
            ).start()

    wait_bytes(ns.meta.at[3], ns.recv.at[1])
    items = item_lanes(ns.meta[3], n_dp, n_table)
    ns.item_rows[0:1, :] = items[0]
    ns.item_rows[1:2, :] = items[1]

    wait_bytes(ns.fin_recv, ns.recv.at[5])
    total = ns.fin_recv[0]
    for k in range(1, half_dp):
        total = total + ns.fin_recv[k]
    lane = lax.rem(lax.rem(dp, half_dp) * col_share, 128)
    block = total[:, 0:col_share]
    for at in range(col_share, 128, col_share):
        block = jnp.where(lane == at, total[:, at:at + col_share], block)
    ns.grad_block[...] = block

    wait_bytes(ns.meta.at[0, pl.ds(0, (n_table - 1) * n_dp)], ns.send.at[0])
    wait_bytes(ns.meta.at[2, pl.ds(0, (n_dp - 1) * n_table)], ns.send.at[1])
    to_core.wait_send()
    wait_bytes(ns.x_send.at[pl.ds(0, (nx - 1) * x_rows)], ns.send.at[3])
    if ny > 1:
        wait_bytes(ns.y_send.at[pl.ds(0, (ny - 1) * row_share)], ns.send.at[4])
    for m in range(half_dp):
        target = core * half_dp + m

        @pl.when(target != dp)
        def _():
            wait_bytes(ns.fin_send.at[m * col_share // 128], ns.fin_sem.at[m])
    for half in range(2):
        for path in range(2):
            for hop, (_, size, rows) in enumerate((first[path], second[path])):
                wait_bytes(ns.again.at[path, half, pl.ds(0, (size - 1) * rows)], ns.hop_send.at[path, half, hop])
    for half in range(2):
        for path in range(2):
            wait_bytes(ns.arrived.at[path, :, pl.ds(half * 128, 128)], ns.hop_recv.at[path, half, 1])


def place_kernel(arrived_ref, item_ref, block_ref, out_ref, table_ref, rows, built, load, store):
    copies = [pltpu.make_async_copy(arrived_ref.at[p], rows.at[p], load.at[p]) for p in range(2)]
    for copy in copies:
        copy.start()
    out_ref[...] = block_ref[...]
    blocks = built.shape[0]
    size = ROWS_DEV // blocks
    stores = []
    for b in range(blocks):
        for p in range(2):
            hits = one_hot(size, item_ref[p:p + 1, :] - b * size)
            if b == 0:
                copies[p].wait()
            built[b, :, 256 - p * 256:512 - p * 256] = dot_nn(hits, rows[p]).astype(BF16)
        stores.append(pltpu.make_async_copy(built.at[b], table_ref.at[pl.ds(b * size, size)], store.at[b]))
        stores[-1].start()
    for copy in stores:
        copy.wait()


INPUTS = ("events", "upstream", "w_in", "w_out", "lengths", "owners", "items")
OUTPUTS = ("grad_block", "item_rows", "arrived")


def scratch(n_dp, n_table):
    row_share = D // n_table
    pairs = n_dp * n_table
    vmem = pltpu.VMEM
    dma = pltpu.SemaphoreType.DMA
    return dict(
        events_v=vmem((TOK, D), BF16),
        upstream_v=vmem((TOK, D), BF16),
        w_in_v=vmem((D + 16, 4 * D), BF16),
        half=vmem((4 * D, TOK), F32),
        upt=vmem((D, TOK), BF16),
        dot=vmem((1, TOK), F32),
        stat=vmem((8, TOK), F32),
        w_out_v=vmem((D, D), BF16),
        bias=vmem((TOK, TOK), F32),
        xnt=vmem((D, TOK), F32),
        normedt=vmem((D, TOK), BF16),
        inv=vmem((1, TOK), F32),
        slope=vmem((4 * D, TOK), F32),
        act=vmem((4 * D, TOK), BF16),
        w=vmem((HEADS, TOK, TOK), BF16),
        dsl=vmem((HEADS, TOK, TOK), F32),
        att=vmem((D, TOK), F32),
        ainv=vmem((1, TOK), F32),
        gated=vmem((D, TOK), BF16),
        zg=vmem((4 * D, TOK), BF16),
        ag=vmem((D, TOK), BF16),
        ds=vmem((TOK, TOK), BF16),
        oh_a=vmem((SLOTS, TOK), BF16),
        oh_b=vmem((SLOTS, TOK), BF16),
        swap_a=vmem((SLOTS, SLOTS), BF16),
        swap_b=vmem((SLOTS, SLOTS), BF16),
        meta=vmem((4, pairs, 128), BF16),
        moved=vmem((2, SLOTS, 256), BF16),
        landed=vmem((2, 2, SLOTS, 128), BF16),
        again=vmem((2, 2, SLOTS, 128), BF16),
        part=vmem((2, D, 256), F32),
        other=vmem((D, 256), F32),
        x_send=vmem((D, 256), BF16),
        x_recv=vmem((D, 256), BF16),
        y_send=vmem((D // 4, 256), BF16),
        y_recv=vmem((D // 4, 256), BF16),
        fin_send=vmem((2, row_share, 128), F32),
        fin_recv=vmem((n_dp // 2, row_share, 128), F32),
        load=dma((4,)),
        send=dma((6,)),
        recv=dma((6,)),
        hop_send=dma((2, 2, 2)),
        hop_recv=dma((2, 2, 2)),
        fin_sem=dma((n_dp // 2,)),
    )


def solution(mesh):
    n_dp, n_table = mesh.shape["dp"], mesh.shape["table"]
    in_vmem = pl.BlockSpec(memory_space=pltpu.VMEM)
    in_smem = pl.BlockSpec(memory_space=pltpu.SMEM)
    anywhere = pl.BlockSpec(memory_space=pl.ANY)

    def local(events, upstream, w_in, w_out, lengths, owners, item_rows):
        block = jax.ShapeDtypeStruct((D // n_table, D // n_dp), F32)
        grad_block, items, arrived = pl.pallas_call(
            functools.partial(kernel, n_dp, n_table),
            out_shape=(
                block,
                jax.ShapeDtypeStruct((8, SLOTS), jnp.int32),
                jax.ShapeDtypeStruct((2, SLOTS, 256), BF16),
            ),
            in_specs=[anywhere] * 4 + [in_smem] + [in_vmem] * 2,
            out_specs=(in_vmem, in_vmem, anywhere),
            scratch_shapes=list(scratch(n_dp, n_table).values()),
            compiler_params=pltpu.CompilerParams(
                collective_id=0, has_side_effects=True, vmem_limit_bytes=60 << 20
            ),
        )(events, upstream, w_in, w_out, lengths, owners.reshape(1, TOK), item_rows.reshape(1, TOK))
        return pl.pallas_call(
            place_kernel,
            out_shape=(block, jax.ShapeDtypeStruct((ROWS_DEV, D), BF16)),
            in_specs=[anywhere, in_vmem, in_vmem],
            out_specs=(in_vmem, anywhere),
            scratch_shapes=[
                pltpu.VMEM((2, SLOTS, 256), BF16),
                pltpu.VMEM((PLACE_BLOCKS, ROWS_DEV // PLACE_BLOCKS, D), BF16),
                pltpu.SemaphoreType.DMA((2,)),
                pltpu.SemaphoreType.DMA((PLACE_BLOCKS,)),
            ],
            compiler_params=pltpu.CompilerParams(vmem_limit_bytes=60 << 20),
        )(arrived, items, grad_block)

    both = P(("dp", "table"), None)
    return jax.shard_map(
        local,
        mesh=mesh,
        in_specs=(both, both, P(), P(), both, both, P(("dp", "table"))),
        out_specs=(P("table", "dp"), both),
        check_vma=False,
    )
```

```python
import functools
import jax
import jax.numpy as jnp
from jax import lax
from jax.experimental import pallas as pl
from jax.experimental.pallas import tpu as pltpu
from jax.sharding import PartitionSpec as P

HEADS = 8
HD = 64
TOK = 512
D = 512
EPS = 1e-6
F32 = jnp.float32
BF16 = jnp.bfloat16
JB = 128
OUT_OF_MASK = -1e30


def dot_nn(a, b):
    return lax.dot_general(a, b, (((1,), (0,)), ((), ())), preferred_element_type=F32)


def dot_nt(a, b):
    return lax.dot_general(a, b, (((1,), (1,)), ((), ())), preferred_element_type=F32)


def window(jb):
    lo = jb * JB
    return lo, min(TOK, -(-(lo + JB + 255) // 128) * 128)


def build_bias(len_ref, bias_ref):
    lengths = len_ref[...]
    upto = lax.broadcasted_iota(jnp.int32, (8, 8), 1) <= lax.broadcasted_iota(jnp.int32, (8, 8), 0)
    ends = jnp.sum(jnp.where(upto, lengths.astype(F32), 0.0), axis=1, keepdims=True).astype(jnp.int32)
    col = lax.broadcasted_iota(jnp.int32, (TOK, 1), 0)
    row = lax.broadcasted_iota(jnp.int32, (1, TOK), 1)
    seg_row = jnp.sum(jnp.where(row >= ends, 1.0, 0.0), axis=0, keepdims=True)
    seg_col = jnp.broadcast_to(seg_row, (128, TOK)).T[:, 0:1]
    for jb in range(TOK // JB):
        lo, hi = window(jb)
        keep = (seg_col[lo:lo + JB] == seg_row[:, lo:hi]) & (col[lo:lo + JB] <= row[:, lo:hi])
        bias_ref[lo:lo + JB, lo:hi] = jnp.where(keep, 0.0, OUT_OF_MASK)


def zero_corners(ref, lead):
    zeros = jnp.zeros(lead + (128, 128), ref.dtype)
    full = (slice(None),) * len(lead)
    ref[full + (slice(0, 128), slice(384, 512))] = zeros
    ref[full + (slice(128, 256), slice(0, 128))] = zeros
    ref[full + (slice(384, 512), slice(256, 384))] = zeros


def normalize_events(ev_ref, xnt_ref, normedt_ref, inv_ref):
    x = ev_ref[...].T.astype(F32)
    mean = jnp.mean(x, axis=0, keepdims=True)
    c = x - mean
    inv = lax.rsqrt(jnp.mean(c * c, axis=0, keepdims=True) + EPS)
    xn = c * inv
    xnt_ref[...] = xn
    normedt_ref[...] = xn.astype(BF16)
    inv_ref[...] = inv


def project(w_in_ref, normedt_ref, slope_ref, act_ref, half_ref):
    for c in range(16):
        lo = c * 128
        wt = w_in_ref[0:D, lo:lo + 128].T
        half = dot_nn(wt, normedt_ref[...]) * 0.5
        half_ref[lo:lo + 128, :] = half
        t = jnp.tanh(half)
        p = 1.0 + t
        act = half * p
        slope_ref[lo:lo + 128, :] = p + act * (1.0 - t)
        act_ref[lo:lo + 128, :] = act.astype(BF16)


def natural(act_ref, nat_ref):
    nat_ref[:, 0:512] = act_ref[512:1024, :].T
    nat_ref[:, 512:1024] = act_ref[1536:2048, :].T


def head_pair_cols(nat_ref, base, pair):
    return nat_ref[:, pl.ds(pl.multiple_of(base + pair * 128, 128), 128)]


def attend_head(h, act_ref, bias_ref, w_ref, dsl_ref, att_ref):
    r = pl.multiple_of(h * HD, HD)
    qt = act_ref[pl.ds(1024 + r, HD), :] * 0.0625
    kt = act_ref[pl.ds(1536 + r, HD), :]
    vt = act_ref[pl.ds(512 + r, HD), :] * (1.0 / 64.0)
    k = kt.T
    for jb in range(TOK // JB):
        lo, hi = window(jb)
        half = dot_nn(k[lo:lo + JB], qt[:, lo:hi]) + bias_ref[lo:lo + JB, lo:hi]
        t = jnp.tanh(half)
        p = 1.0 + t
        w = half * p
        w_ref[h, lo:lo + JB, lo:hi] = w.astype(BF16)
        dsl_ref[h, lo:lo + JB, lo:hi] = p + w * (1.0 - t)
    att_ref[pl.ds(r, HD), 0:256] = dot_nn(vt[:, 0:256], w_ref[h, 0:256, 0:256])
    att_ref[pl.ds(r, HD), 256:512] = dot_nn(vt, w_ref[h, :, 256:512])


def norm_att(att_ref, ainv_ref, act_ref, gated_ref):
    a = att_ref[...]
    mean = jnp.mean(a, axis=0, keepdims=True)
    c = a - mean
    inv = lax.rsqrt(jnp.mean(c * c, axis=0, keepdims=True) + EPS)
    an = c * inv
    att_ref[...] = an
    ainv_ref[...] = inv
    gated_ref[...] = (an * act_ref[0:512, :].astype(F32)).astype(BF16)


def put_z_grad(at, lanes, joined, slope_ref, half_ref, zg_ref, dot_ref):
    grad = (joined * slope_ref[at, lanes]).astype(BF16)
    zg_ref[at, lanes] = grad
    dot_ref[:, lanes] += jnp.sum(grad.astype(F32) * half_ref[at, lanes], axis=0, keepdims=True)


def att_backward(w_out_ref, up_ref, upt_ref, att_ref, ainv_ref, act_ref, ag_ref, z_refs):
    upt_ref[...] = up_ref[...].T
    gg = dot_nn(w_out_ref[...], upt_ref[...])
    an = att_ref[...]
    put_z_grad(slice(0, 512), slice(0, 512), gg * an, *z_refs)
    g = gg * act_ref[0:512, :].astype(F32)
    first = jnp.mean(g, axis=0, keepdims=True)
    second = jnp.mean(g * an, axis=0, keepdims=True)
    ag_ref[...] = ((g - first - an * second) * (ainv_ref[...] * (1.0 / 128.0))).astype(BF16)


def backward_head(h, act_ref, ag_ref, w_ref, dsl_ref, ds_ref, z_refs):
    r = h * HD
    qt = act_ref[1024 + r:1024 + r + HD, :]
    kt = act_ref[1536 + r:1536 + r + HD, :]
    v = act_ref[512 + r:512 + r + HD, :].T
    ag = ag_ref[r:r + HD, :]
    for jb in range(TOK // JB):
        lo, hi = window(jb)
        wg = dot_nn(v[lo:lo + JB], ag[:, lo:hi])
        ds_ref[lo:lo + JB, lo:hi] = (wg * dsl_ref[h, lo:lo + JB, lo:hi]).astype(BF16)
    left, right = slice(0, 256), slice(256, 512)
    rows = [slice(base + r, base + r + HD) for base in (512, 1024, 1536)]
    put_z_grad(rows[0], left, dot_nt(ag, w_ref[h, 0:256, :]) * 2.0, *z_refs)
    put_z_grad(rows[0], right, dot_nt(ag[:, right], w_ref[h, right, right]) * 2.0, *z_refs)
    put_z_grad(rows[1], left, dot_nn(kt[:, left], ds_ref[left, left]) * 0.125, *z_refs)
    put_z_grad(rows[1], right, dot_nn(kt, ds_ref[:, right]) * 0.125, *z_refs)
    put_z_grad(rows[2], left, dot_nt(qt, ds_ref[left, :]) * 0.125, *z_refs)
    put_z_grad(rows[2], right, dot_nt(qt[:, right], ds_ref[right, right]) * 0.125, *z_refs)


def sum_rows(w_in_ref):
    sums = dot_nn(jnp.ones((8, D), BF16), w_in_ref[0:D, :])
    high = sums.astype(BF16)
    w_in_ref[D:D + 16, :] = jnp.concatenate([high, (sums - high.astype(F32)).astype(BF16)], axis=0)


def event_gradient(path, w_in_ref, zg_ref, dot_ref, stat_ref, upt_ref, xnt_ref, inv_ref):
    if path == 0:
        ng = dot_nn(w_in_ref[256:D + 16, :], zg_ref[...])
        stat_ref[0:1, :] = (ng[256:257] + ng[264:265]) * (1.0 / 512.0)
        stat_ref[1:2, :] = dot_ref[...] * (1.0 / 256.0)
        ng = ng[0:256]
        at = slice(256, 512)
    else:
        at = slice(0, 256)
        ng = dot_nn(w_in_ref[at, :], zg_ref[...])
    back = (ng - stat_ref[0:1, :] - xnt_ref[at, :] * stat_ref[1:2, :]) * (inv_ref[...] * 0.5)
    return (upt_ref[at, :].astype(F32) + back).astype(BF16)


MESH = pl.DeviceIdType.MESH
SLOTS = 1024
ROWS_DEV = 1024
PLACE_BLOCKS = 4


def log2(n):
    return n.bit_length() - 1


def one_hot(rows, cols_of):
    at = lax.broadcasted_iota(jnp.int32, (rows, cols_of.shape[1]), 0)
    return jnp.where(at == cols_of, 1.0, 0.0).astype(BF16)


def block_at(n, rows):
    return pl.ds(pl.multiple_of(n * rows, rows), rows) if rows > 1 else pl.ds(n, 1)


def start_all(axis, size, rows, src_ref, dst_ref, send_sem, recv_sem, lo=0, step=1):
    at = lax.axis_index(axis)
    me = lax.div(at - lo, step)
    mine = block_at(me, rows)
    pltpu.make_async_copy(src_ref.at[mine], dst_ref.at[mine], recv_sem).start()

    def send(k, carry):
        peer = lax.rem(me + k, size)
        pltpu.make_async_remote_copy(
            src_ref=src_ref.at[block_at(peer, rows)],
            dst_ref=dst_ref.at[mine],
            send_sem=send_sem,
            recv_sem=recv_sem,
            device_id={axis: lo + peer * step},
            device_id_type=MESH,
        ).start()
        return carry

    lax.fori_loop(1, size, send, 0)


def wait_bytes(ref, sem):
    pltpu.make_async_copy(ref, ref, sem).wait()


def route_slots(owner_ref, item_ref, n_dp, n_table, oh_a, oh_b, meta_ref):
    pairs = n_dp * n_table
    cap = SLOTS // pairs
    row = owner_ref[...]
    col = jnp.broadcast_to(row, (128, TOK)).T[:, 0:1]
    place_col = lax.broadcasted_iota(jnp.int32, (TOK, 1), 0)
    place_row = lax.broadcasted_iota(jnp.int32, (1, TOK), 1)
    earlier = (col == row) & (place_col < place_row)
    rank = jnp.sum(jnp.where(earlier, 1.0, 0.0), axis=0, keepdims=True).astype(jnp.int32)
    table, dp = row & (n_table - 1), row >> log2(n_table)
    oh_a[...] = one_hot(SLOTS, table * (n_dp * cap) + dp * cap + rank)
    oh_b[...] = one_hot(SLOTS, dp * (n_table * cap) + table * cap + rank)
    code = item_ref[...] + 1
    to_table = one_hot(n_table, table).astype(F32)
    lane = one_hot(meta_ref.shape[1], dp * cap + rank)
    high, low = (dot_nt((to_table * word.astype(F32)).astype(BF16), lane) for word in (code >> 5, code & 31))
    meta_ref[...] = high * 32.0 + low


def words(values):
    whole = values.astype(jnp.int32)
    return (whole >> 5).astype(F32).astype(BF16), (whole & 31).astype(F32).astype(BF16)


def turn_items(landed, n_dp, cap):
    n_table, lanes = landed.shape
    row = lax.broadcasted_iota(jnp.int32, (lanes, 1), 0)
    col = lax.broadcasted_iota(jnp.int32, (1, lanes), 1)
    spread = one_hot(n_table, col >> log2(cap))
    gather = jnp.where((lax.broadcasted_iota(jnp.int32, (n_dp, lanes), 0)) == (
        lax.broadcasted_iota(jnp.int32, (n_dp, lanes), 1) >> log2(cap)), 1.0, 0.0).astype(BF16)
    parts = []
    for word in words(landed):
        turned = dot_nn(word.astype(F32).T.astype(BF16), spread)
        kept = jnp.where((row & (cap - 1)) == (col & (cap - 1)), turned, 0.0).astype(BF16)
        parts.append(dot_nn(gather, kept))
    return parts[0] * 32.0 + parts[1]


def swap_rows(first, second, cap):
    n = first * second * cap
    out = lax.broadcasted_iota(jnp.int32, (n, 1), 0)
    slot = out & (cap - 1)
    a = (out >> log2(cap)) & (first - 1)
    b = out >> (log2(cap) + log2(first))
    at = lax.broadcasted_iota(jnp.int32, (n, n), 1)
    return jnp.where(at == a * (second * cap) + b * cap + slot, 1.0, 0.0).astype(BF16)


def item_lanes(turned, n_dp, n_table):
    cap = SLOTS // (n_dp * n_table)
    col = lax.broadcasted_iota(jnp.int32, (1, SLOTS), 1)
    row = lax.broadcasted_iota(jnp.int32, (n_dp, SLOTS), 0)
    slot, pair = col & (cap - 1), col >> log2(cap)
    high, low = words(turned)
    items = []
    for dp, table in ((pair >> log2(n_table), pair & (n_table - 1)), (pair & (n_dp - 1), pair >> log2(n_dp))):
        spread = one_hot(turned.shape[1], table * cap + slot)
        every = dot_nn(high, spread) * 32.0 + dot_nn(low, spread)
        items.append((jnp.sum(jnp.where(row == dp, every, 0.0), axis=0, keepdims=True) - 1.0).astype(jnp.int32))
    return items


def kernel(n_dp, n_table, *refs):
    names = INPUTS + OUTPUTS + tuple(scratch(n_dp, n_table))
    ns = type("Refs", (), dict(zip(names, refs)))
    dp, table = lax.axis_index("dp"), lax.axis_index("table")
    core = lax.rem(dp, 2)
    pairs = n_dp * n_table
    cap = SLOTS // pairs
    nx = 4
    ny = n_table // nx
    row_share, col_share, half_dp = D // n_table, D // n_dp, n_dp // 2
    x_rows = ny * row_share

    loads = {}
    for n, name in enumerate(INPUTS):
        held = getattr(ns, name + "_v")
        held = held.at[pl.ds(0, D)] if name == "w_in" else held
        loads[name] = pltpu.make_async_copy(getattr(ns, name), held, ns.load.at[n])
        loads[name].start()

    barrier = pltpu.get_barrier_semaphore()
    for axis, size, me in (("table", n_table, table), ("dp", n_dp, dp)):
        def greet(k, carry, axis=axis, size=size, me=me):
            pl.semaphore_signal(
                barrier, inc=1, device_id={axis: lax.rem(me + k, size)}, device_id_type=MESH
            )
            return carry
        lax.fori_loop(1, size, greet, 0)

    zero_corners(ns.w, (HEADS,))
    zero_corners(ns.ds, ())
    loads["lengths"].wait()
    build_bias(ns.lengths_v, ns.bias)
    loads["events"].wait()
    normalize_events(ns.events_v, ns.xnt, ns.normedt, ns.inv)
    loads["owners"].wait()
    loads["items"].wait()
    route_slots(ns.owners_v, ns.items_v, n_dp, n_table, ns.oh_a, ns.oh_b, ns.item_send)
    loads["w_in"].wait()
    project(ns.w_in_v, ns.normedt, ns.slope, ns.act, ns.half)
    sum_rows(ns.w_in_v)

    for h in range(HEADS):
        attend_head(h, ns.act, ns.bias, ns.w, ns.dsl, ns.att)
    norm_att(ns.att, ns.ainv, ns.act, ns.gated)
    loads["upstream"].wait()
    for half in range(2):
        ns.part[half] = dot_nn(ns.gated[...], ns.upstream_v[:, half * 256:half * 256 + 256])
    pl.semaphore_wait(barrier, n_table + n_dp - 2)
    start_all("table", n_table, 1, ns.item_send, ns.item_land, ns.send.at[0], ns.recv.at[0])
    to_core = pltpu.make_async_remote_copy(
        src_ref=ns.part.at[1 - core],
        dst_ref=ns.other,
        send_sem=ns.send.at[2],
        recv_sem=ns.recv.at[2],
        device_id={"dp": dp + 1 - 2 * core},
        device_id_type=MESH,
    )
    to_core.start()
    loads["w_out"].wait()
    ns.dot[...] = jnp.zeros_like(ns.dot)
    z_refs = (ns.slope, ns.half, ns.zg, ns.dot)
    att_backward(ns.w_out_v, ns.upstream_v, ns.upt, ns.att, ns.ainv, ns.act, ns.ag, z_refs)
    for h in range(HEADS):
        backward_head(h, ns.act, ns.ag, ns.w, ns.dsl, ns.ds, z_refs)
        if h == 5:
            to_core.wait_recv()
            for t in range(n_table):
                y, x = t // nx, t % nx
                rows = slice(t * row_share, (t + 1) * row_share)
                ns.x_send[x * x_rows + y * row_share:x * x_rows + (y + 1) * row_share] = (
                    ns.part[core, rows] + ns.other[rows]
                ).astype(BF16)
            start_all("table", nx, x_rows, ns.x_send, ns.x_recv, ns.send.at[3], ns.recv.at[3], lo=lax.div(table, nx) * nx)

    first = (("table", n_table, n_dp * cap), ("dp", n_dp, n_table * cap))
    second = first[::-1]

    def hop_one(path, half):
        lanes = pl.ds(half * 128, 128)
        start_all(
            *first[path], ns.moved.at[path, :, lanes], ns.landed.at[path, half],
            ns.hop_send.at[path, half, 0], ns.hop_recv.at[path, half, 0],
        )

    def hop_two(path, half):
        swap = (ns.swap_a, ns.swap_b)[path]
        wait_bytes(ns.landed.at[path, half], ns.hop_recv.at[path, half, 0])
        ns.again[path, half] = dot_nn(swap[...], ns.landed[path, half]).astype(BF16)
        start_all(
            *second[path], ns.again.at[path, half], ns.arrived.at[path, :, pl.ds(half * 128, 128)],
            ns.hop_send.at[path, half, 1], ns.hop_recv.at[path, half, 1],
        )

    for path, slots in ((0, ns.oh_a), (1, ns.oh_b)):
        grad = event_gradient(path, ns.w_in_v, ns.zg, ns.dot, ns.stat, ns.upt, ns.xnt, ns.inv)
        ns.moved[path] = dot_nt(slots[...], grad).astype(BF16)
        hop_one(path, 0)
    hop_one(0, 1)
    hop_one(1, 1)

    wait_bytes(ns.item_land, ns.recv.at[0])
    ns.item_again[...] = turn_items(ns.item_land[...], n_dp, cap)
    start_all("dp", n_dp, 1, ns.item_again, ns.item_done, ns.send.at[1], ns.recv.at[1])
    ns.swap_a[...] = swap_rows(n_table, n_dp, cap)
    ns.swap_b[...] = swap_rows(n_dp, n_table, cap)

    wait_bytes(ns.x_recv, ns.recv.at[3])
    share = ns.x_recv[0:x_rows].astype(F32)
    for x in range(1, nx):
        share = share + ns.x_recv[x * x_rows:(x + 1) * x_rows].astype(F32)
    ns.y_send[...] = share.astype(BF16)
    start_all("table", ny, row_share, ns.y_send, ns.y_recv, ns.send.at[4], ns.recv.at[4], lo=lax.rem(table, nx), step=nx)

    hop_two(0, 0)
    hop_two(1, 0)

    hop_two(0, 1)
    hop_two(1, 1)

    wait_bytes(ns.y_recv, ns.recv.at[4])
    share = ns.y_recv[0:row_share].astype(F32)
    for y in range(1, ny):
        share = share + ns.y_recv[y * row_share:(y + 1) * row_share].astype(F32)
    for g in range(2):
        ns.fin_send[g] = share[:, g * 128:g * 128 + 128]
    z = lax.div(dp, 2)
    for m in range(half_dp):
        target = core * half_dp + m
        group = ns.fin_send.at[m * col_share // 128]

        @pl.when(target == dp)
        def _():
            pltpu.make_async_copy(group, ns.fin_recv.at[z], ns.recv.at[5]).start()

        @pl.when(target != dp)
        def _():
            pltpu.make_async_remote_copy(
                src_ref=group,
                dst_ref=ns.fin_recv.at[z],
                send_sem=ns.fin_sem.at[m],
                recv_sem=ns.recv.at[5],
                device_id={"dp": target},
                device_id_type=MESH,
            ).start()

    wait_bytes(ns.item_done, ns.recv.at[1])
    items = item_lanes(ns.item_done[...], n_dp, n_table)
    ns.item_rows[0:1, :] = items[0]
    ns.item_rows[1:2, :] = items[1]

    wait_bytes(ns.fin_recv, ns.recv.at[5])
    total = ns.fin_recv[0]
    for k in range(1, half_dp):
        total = total + ns.fin_recv[k]
    lane = lax.rem(lax.rem(dp, half_dp) * col_share, 128)
    block = total[:, 0:col_share]
    for at in range(col_share, 128, col_share):
        block = jnp.where(lane == at, total[:, at:at + col_share], block)
    ns.grad_block[...] = block

    wait_bytes(ns.item_send.at[pl.ds(0, n_table - 1)], ns.send.at[0])
    wait_bytes(ns.item_again.at[pl.ds(0, n_dp - 1)], ns.send.at[1])
    to_core.wait_send()
    wait_bytes(ns.x_send.at[pl.ds(0, (nx - 1) * x_rows)], ns.send.at[3])
    if ny > 1:
        wait_bytes(ns.y_send.at[pl.ds(0, (ny - 1) * row_share)], ns.send.at[4])
    for m in range(half_dp):
        target = core * half_dp + m

        @pl.when(target != dp)
        def _():
            wait_bytes(ns.fin_send.at[m * col_share // 128], ns.fin_sem.at[m])
    for half in range(2):
        for path in range(2):
            for hop, (_, size, rows) in enumerate((first[path], second[path])):
                wait_bytes(ns.again.at[path, half, pl.ds(0, (size - 1) * rows)], ns.hop_send.at[path, half, hop])
    for half in range(2):
        for path in range(2):
            wait_bytes(ns.arrived.at[path, :, pl.ds(half * 128, 128)], ns.hop_recv.at[path, half, 1])


def place_kernel(arrived_ref, item_ref, block_ref, out_ref, table_ref, rows, items, built, load, store):
    copies = [pltpu.make_async_copy(item_ref, items, load.at[2])]
    copies += [pltpu.make_async_copy(arrived_ref.at[p], rows.at[p], load.at[p]) for p in range(2)]
    block_copy = pltpu.make_async_copy(block_ref, out_ref, load.at[3])
    for copy in copies:
        copy.start()
    block_copy.start()
    copies[0].wait()
    blocks = built.shape[0]
    size = ROWS_DEV // blocks
    stores = []
    for b in range(blocks):
        for p in range(2):
            hits = one_hot(size, items[p:p + 1, :] - b * size)
            if b == 0:
                copies[p + 1].wait()
            built[b, :, 256 - p * 256:512 - p * 256] = dot_nn(hits, rows[p]).astype(BF16)
        stores.append(pltpu.make_async_copy(built.at[b], table_ref.at[pl.ds(b * size, size)], store.at[b]))
        stores[-1].start()
    block_copy.wait()
    for copy in stores:
        copy.wait()


INPUTS = ("events", "lengths", "owners", "items", "w_in", "upstream", "w_out")
OUTPUTS = ("grad_block", "item_rows", "arrived")


def scratch(n_dp, n_table):
    row_share = D // n_table
    item_lane = max(128, SLOTS // min(n_dp, n_table))
    vmem = pltpu.VMEM
    dma = pltpu.SemaphoreType.DMA
    return dict(
        events_v=vmem((TOK, D), BF16),
        lengths_v=vmem((1, 8), jnp.int32),
        owners_v=vmem((1, TOK), jnp.int32),
        items_v=vmem((1, TOK), jnp.int32),
        upstream_v=vmem((TOK, D), BF16),
        w_in_v=vmem((D + 16, 4 * D), BF16),
        half=vmem((4 * D, TOK), F32),
        upt=vmem((D, TOK), BF16),
        dot=vmem((1, TOK), F32),
        stat=vmem((8, TOK), F32),
        w_out_v=vmem((D, D), BF16),
        bias=vmem((TOK, TOK), F32),
        xnt=vmem((D, TOK), F32),
        normedt=vmem((D, TOK), BF16),
        inv=vmem((1, TOK), F32),
        slope=vmem((4 * D, TOK), F32),
        act=vmem((4 * D, TOK), BF16),
        w=vmem((HEADS, TOK, TOK), BF16),
        dsl=vmem((HEADS, TOK, TOK), F32),
        att=vmem((D, TOK), F32),
        ainv=vmem((1, TOK), F32),
        gated=vmem((D, TOK), BF16),
        zg=vmem((4 * D, TOK), BF16),
        ag=vmem((D, TOK), BF16),
        ds=vmem((TOK, TOK), BF16),
        oh_a=vmem((SLOTS, TOK), BF16),
        oh_b=vmem((SLOTS, TOK), BF16),
        swap_a=vmem((SLOTS, SLOTS), BF16),
        swap_b=vmem((SLOTS, SLOTS), BF16),
        item_send=vmem((n_table, item_lane), F32),
        item_land=vmem((n_table, item_lane), F32),
        item_again=vmem((n_dp, item_lane), F32),
        item_done=vmem((n_dp, item_lane), F32),
        moved=vmem((2, SLOTS, 256), BF16),
        landed=vmem((2, 2, SLOTS, 128), BF16),
        again=vmem((2, 2, SLOTS, 128), BF16),
        part=vmem((2, D, 256), F32),
        other=vmem((D, 256), F32),
        x_send=vmem((D, 256), BF16),
        x_recv=vmem((D, 256), BF16),
        y_send=vmem((D // 4, 256), BF16),
        y_recv=vmem((D // 4, 256), BF16),
        fin_send=vmem((2, row_share, 128), F32),
        fin_recv=vmem((n_dp // 2, row_share, 128), F32),
        load=dma((len(INPUTS),)),
        send=dma((6,)),
        recv=dma((6,)),
        hop_send=dma((2, 2, 2)),
        hop_recv=dma((2, 2, 2)),
        fin_sem=dma((n_dp // 2,)),
    )


def solution(mesh):
    n_dp, n_table = mesh.shape["dp"], mesh.shape["table"]
    in_vmem = pl.BlockSpec(memory_space=pltpu.VMEM)
    anywhere = pl.BlockSpec(memory_space=pl.ANY)

    def local(events, upstream, w_in, w_out, lengths, owners, item_rows):
        block = jax.ShapeDtypeStruct((D // n_table, D // n_dp), F32)
        grad_block, items, arrived = pl.pallas_call(
            functools.partial(kernel, n_dp, n_table),
            out_shape=(
                block,
                jax.ShapeDtypeStruct((8, SLOTS), jnp.int32),
                jax.ShapeDtypeStruct((2, SLOTS, 256), BF16),
            ),
            in_specs=[anywhere] * len(INPUTS),
            out_specs=(in_vmem, in_vmem, anywhere),
            scratch_shapes=list(scratch(n_dp, n_table).values()),
            compiler_params=pltpu.CompilerParams(
                collective_id=0, has_side_effects=True, vmem_limit_bytes=60 << 20
            ),
        )(events, lengths, owners.reshape(1, TOK), item_rows.reshape(1, TOK), w_in, upstream, w_out)
        return pl.pallas_call(
            place_kernel,
            out_shape=(block, jax.ShapeDtypeStruct((ROWS_DEV, D), BF16)),
            in_specs=[anywhere] * 3,
            out_specs=(anywhere, anywhere),
            scratch_shapes=[
                pltpu.VMEM((2, SLOTS, 256), BF16),
                pltpu.VMEM((8, SLOTS), jnp.int32),
                pltpu.VMEM((PLACE_BLOCKS, ROWS_DEV // PLACE_BLOCKS, D), BF16),
                pltpu.SemaphoreType.DMA((4,)),
                pltpu.SemaphoreType.DMA((PLACE_BLOCKS,)),
            ],
            compiler_params=pltpu.CompilerParams(vmem_limit_bytes=60 << 20),
        )(arrived, items, grad_block)

    both = P(("dp", "table"), None)
    return jax.shard_map(
        local,
        mesh=mesh,
        in_specs=(both, both, P(), P(), both, both, P(("dp", "table"))),
        out_specs=(P("table", "dp"), both),
        check_vma=False,
    )
```

```python
import functools
import jax
import jax.numpy as jnp
from jax import lax
from jax.experimental import pallas as pl
from jax.experimental.pallas import tpu as pltpu
from jax.sharding import PartitionSpec as P

HEADS = 8
HD = 64
TOK = 512
D = 512
EPS = 1e-6
F32 = jnp.float32
BF16 = jnp.bfloat16
JB = 256
OUT_OF_MASK = -1e30


def dot_nn(a, b):
    return lax.dot_general(a, b, (((1,), (0,)), ((), ())), preferred_element_type=F32)


def dot_nt(a, b):
    return lax.dot_general(a, b, (((1,), (1,)), ((), ())), preferred_element_type=F32)


def window(jb):
    lo = jb * JB
    return lo, min(TOK, -(-(lo + JB + 255) // 128) * 128)


def build_bias(len_ref, bias_ref):
    lengths = len_ref[...]
    upto = lax.broadcasted_iota(jnp.int32, (8, 8), 1) <= lax.broadcasted_iota(jnp.int32, (8, 8), 0)
    ends = jnp.sum(jnp.where(upto, lengths.astype(F32), 0.0), axis=1, keepdims=True).astype(jnp.int32)
    col = lax.broadcasted_iota(jnp.int32, (TOK, 1), 0)
    row = lax.broadcasted_iota(jnp.int32, (1, TOK), 1)
    seg_row = jnp.sum(jnp.where(row >= ends, 1.0, 0.0), axis=0, keepdims=True)
    seg_col = jnp.broadcast_to(seg_row, (128, TOK)).T[:, 0:1]
    for jb in range(TOK // JB):
        lo, hi = window(jb)
        keep = (seg_col[lo:lo + JB] == seg_row[:, lo:hi]) & (col[lo:lo + JB] <= row[:, lo:hi])
        bias_ref[lo:lo + JB, lo:hi] = jnp.where(keep, 0.0, OUT_OF_MASK)


def normalize_events(ev_ref, xnt_ref, normedt_ref, inv_ref):
    x = ev_ref[...].T.astype(F32)
    mean = jnp.mean(x, axis=0, keepdims=True)
    c = x - mean
    inv = lax.rsqrt(jnp.mean(c * c, axis=0, keepdims=True) + EPS)
    xn = c * inv
    xnt_ref[...] = xn
    normedt_ref[...] = xn.astype(BF16)
    inv_ref[...] = inv


def project(w_in_ref, normedt_ref, slope_ref, act_ref, half_ref):
    for c in range(16):
        lo = c * 128
        wt = w_in_ref[0:D, lo:lo + 128].T
        half = dot_nn(wt, normedt_ref[...]) * 0.5
        half_ref[lo:lo + 128, :] = half
        t = jnp.tanh(half)
        p = 1.0 + t
        act = half * p
        slope_ref[lo:lo + 128, :] = p + act * (1.0 - t)
        act_ref[lo:lo + 128, :] = act.astype(BF16)


def natural(act_ref, nat_ref):
    nat_ref[:, 0:512] = act_ref[512:1024, :].T
    nat_ref[:, 512:1024] = act_ref[1536:2048, :].T


def head_pair_cols(nat_ref, base, pair):
    return nat_ref[:, pl.ds(pl.multiple_of(base + pair * 128, 128), 128)]


def attend_head(h, act_ref, bias_ref, w_ref, dsl_ref, att_ref):
    r = pl.multiple_of(h * HD, HD)
    qt = act_ref[pl.ds(1024 + r, HD), :] * 0.0625
    kt = act_ref[pl.ds(1536 + r, HD), :]
    vt = act_ref[pl.ds(512 + r, HD), :] * (1.0 / 64.0)
    k = kt.T
    for jb in range(TOK // JB):
        lo, hi = window(jb)
        half = dot_nn(k[lo:lo + JB], qt[:, lo:hi]) + bias_ref[lo:lo + JB, lo:hi]
        t = jnp.tanh(half)
        p = 1.0 + t
        w = half * p
        w_ref[h, lo:lo + JB, lo:hi] = w.astype(BF16)
        dsl_ref[h, lo:lo + JB, lo:hi] = p + w * (1.0 - t)
    att_ref[pl.ds(r, HD), 0:256] = dot_nn(vt[:, 0:256], w_ref[h, 0:256, 0:256])
    att_ref[pl.ds(r, HD), 256:512] = dot_nn(vt, w_ref[h, :, 256:512])


def norm_att(att_ref, ainv_ref, act_ref, gated_ref):
    a = att_ref[...]
    mean = jnp.mean(a, axis=0, keepdims=True)
    c = a - mean
    inv = lax.rsqrt(jnp.mean(c * c, axis=0, keepdims=True) + EPS)
    an = c * inv
    att_ref[...] = an
    ainv_ref[...] = inv
    gated_ref[...] = (an * act_ref[0:512, :].astype(F32)).astype(BF16)


def put_z_grad(at, lanes, joined, slope_ref, half_ref, zg_ref, dot_ref):
    grad = (joined * slope_ref[at, lanes]).astype(BF16)
    zg_ref[at, lanes] = grad
    dot_ref[:, lanes] += jnp.sum(grad.astype(F32) * half_ref[at, lanes], axis=0, keepdims=True)


def att_backward(w_out_ref, up_ref, upt_ref, att_ref, ainv_ref, act_ref, ag_ref, z_refs):
    upt_ref[...] = up_ref[...].T
    gg = dot_nn(w_out_ref[...], upt_ref[...])
    an = att_ref[...]
    put_z_grad(slice(0, 512), slice(0, 512), gg * an, *z_refs)
    g = gg * act_ref[0:512, :].astype(F32)
    first = jnp.mean(g, axis=0, keepdims=True)
    second = jnp.mean(g * an, axis=0, keepdims=True)
    ag_ref[...] = ((g - first - an * second) * (ainv_ref[...] * (1.0 / 128.0))).astype(BF16)


def backward_head(h, act_ref, ag_ref, w_ref, dsl_ref, ds_ref, z_refs):
    r = h * HD
    qt = act_ref[1024 + r:1024 + r + HD, :]
    kt = act_ref[1536 + r:1536 + r + HD, :]
    v = act_ref[512 + r:512 + r + HD, :].T
    ag = ag_ref[r:r + HD, :]
    for jb in range(TOK // JB):
        lo, hi = window(jb)
        wg = dot_nn(v[lo:lo + JB], ag[:, lo:hi])
        ds_ref[lo:lo + JB, lo:hi] = (wg * dsl_ref[h, lo:lo + JB, lo:hi]).astype(BF16)
    left, right = slice(0, 256), slice(256, 512)
    rows = [slice(base + r, base + r + HD) for base in (512, 1024, 1536)]
    put_z_grad(rows[0], left, dot_nt(ag, w_ref[h, 0:256, :]) * 2.0, *z_refs)
    put_z_grad(rows[0], right, dot_nt(ag[:, right], w_ref[h, right, right]) * 2.0, *z_refs)
    put_z_grad(rows[1], left, dot_nn(kt[:, left], ds_ref[left, left]) * 0.125, *z_refs)
    put_z_grad(rows[1], right, dot_nn(kt, ds_ref[:, right]) * 0.125, *z_refs)
    put_z_grad(rows[2], left, dot_nt(qt, ds_ref[left, :]) * 0.125, *z_refs)
    put_z_grad(rows[2], right, dot_nt(qt[:, right], ds_ref[right, right]) * 0.125, *z_refs)


def sum_rows(w_in_ref):
    sums = dot_nn(jnp.ones((8, D), BF16), w_in_ref[0:D, :])
    high = sums.astype(BF16)
    w_in_ref[D:D + 16, :] = jnp.concatenate([high, (sums - high.astype(F32)).astype(BF16)], axis=0)


def event_gradient(part, w_in_ref, zg_ref, dot_ref, stat_ref, upt_ref, xnt_ref, inv_ref):
    if part == 1:
        at = slice(256, 512)
        ng = dot_nn(w_in_ref[256:D + 16, :], zg_ref[...])
        stat_ref[0:1, :] = (ng[256:257] + ng[264:265]) * (1.0 / 512.0)
        stat_ref[1:2, :] = dot_ref[...] * (1.0 / 256.0)
        ng = ng[0:256]
    else:
        at = slice(0, 256)
        ng = dot_nn(w_in_ref[at, :], zg_ref[...])
    back = (ng - stat_ref[0:1, :] - xnt_ref[at, :] * stat_ref[1:2, :]) * (inv_ref[...] * 0.5)
    return (upt_ref[at, :].astype(F32) + back).astype(BF16)


MESH = pl.DeviceIdType.MESH
SLOTS = 1024
ROWS_DEV = 1024
PLACE_BLOCKS = 4


def log2(n):
    return n.bit_length() - 1


def one_hot(rows, cols_of):
    at = lax.broadcasted_iota(jnp.int32, (rows, cols_of.shape[1]), 0)
    return jnp.where(at == cols_of, 1.0, 0.0).astype(BF16)


def block_at(n, rows):
    return pl.ds(pl.multiple_of(n * rows, rows), rows) if rows > 1 else pl.ds(n, 1)


def start_all(axis, size, rows, src_ref, dst_ref, send_sem, recv_sem, lo=0, step=1):
    at = lax.axis_index(axis)
    me = lax.div(at - lo, step)
    mine = block_at(me, rows)
    pltpu.make_async_copy(src_ref.at[mine], dst_ref.at[mine], recv_sem).start()

    def send(k, carry):
        peer = lax.rem(me + k, size)
        pltpu.make_async_remote_copy(
            src_ref=src_ref.at[block_at(peer, rows)],
            dst_ref=dst_ref.at[mine],
            send_sem=send_sem,
            recv_sem=recv_sem,
            device_id={axis: lo + peer * step},
            device_id_type=MESH,
        ).start()
        return carry

    lax.fori_loop(1, size, send, 0)


def wait_bytes(ref, sem):
    pltpu.make_async_copy(ref, ref, sem).wait()


def route_slots(owner_ref, item_ref, n_dp, n_table, oh_a, oh_b, meta_ref):
    pairs = n_dp * n_table
    cap = SLOTS // pairs
    row = owner_ref[...]
    col = jnp.broadcast_to(row, (128, TOK)).T[:, 0:1]
    place_col = lax.broadcasted_iota(jnp.int32, (TOK, 1), 0)
    place_row = lax.broadcasted_iota(jnp.int32, (1, TOK), 1)
    earlier = (col == row) & (place_col < place_row)
    rank = jnp.sum(jnp.where(earlier, 1.0, 0.0), axis=0, keepdims=True).astype(jnp.int32)
    table, dp = row & (n_table - 1), row >> log2(n_table)
    oh_a[...] = one_hot(SLOTS, table * (n_dp * cap) + dp * cap + rank)
    oh_b[...] = one_hot(SLOTS, dp * (n_table * cap) + table * cap + rank)
    code = item_ref[...] + 1
    to_table = one_hot(n_table, table).astype(F32)
    lane = one_hot(meta_ref.shape[1], dp * cap + rank)
    high, low = (dot_nt((to_table * word.astype(F32)).astype(BF16), lane) for word in (code >> 5, code & 31))
    meta_ref[...] = high * 32.0 + low


def words(values):
    whole = values.astype(jnp.int32)
    return (whole >> 5).astype(F32).astype(BF16), (whole & 31).astype(F32).astype(BF16)


def turn_items(landed, n_dp, cap):
    n_table, lanes = landed.shape
    row = lax.broadcasted_iota(jnp.int32, (lanes, 1), 0)
    col = lax.broadcasted_iota(jnp.int32, (1, lanes), 1)
    spread = one_hot(n_table, col >> log2(cap))
    gather = jnp.where((lax.broadcasted_iota(jnp.int32, (n_dp, lanes), 0)) == (
        lax.broadcasted_iota(jnp.int32, (n_dp, lanes), 1) >> log2(cap)), 1.0, 0.0).astype(BF16)
    parts = []
    for word in words(landed):
        turned = dot_nn(word.astype(F32).T.astype(BF16), spread)
        kept = jnp.where((row & (cap - 1)) == (col & (cap - 1)), turned, 0.0).astype(BF16)
        parts.append(dot_nn(gather, kept))
    return parts[0] * 32.0 + parts[1]


def swap_rows(first, second, cap):
    n = first * second * cap
    out = lax.broadcasted_iota(jnp.int32, (n, 1), 0)
    slot = out & (cap - 1)
    a = (out >> log2(cap)) & (first - 1)
    b = out >> (log2(cap) + log2(first))
    at = lax.broadcasted_iota(jnp.int32, (n, n), 1)
    return jnp.where(at == a * (second * cap) + b * cap + slot, 1.0, 0.0).astype(BF16)


def item_lanes(turned, n_dp, n_table):
    cap = SLOTS // (n_dp * n_table)
    col = lax.broadcasted_iota(jnp.int32, (1, SLOTS), 1)
    row = lax.broadcasted_iota(jnp.int32, (n_dp, SLOTS), 0)
    slot, pair = col & (cap - 1), col >> log2(cap)
    high, low = words(turned)
    items = []
    for dp, table in ((pair >> log2(n_table), pair & (n_table - 1)), (pair & (n_dp - 1), pair >> log2(n_dp))):
        spread = one_hot(turned.shape[1], table * cap + slot)
        every = dot_nn(high, spread) * 32.0 + dot_nn(low, spread)
        items.append((jnp.sum(jnp.where(row == dp, every, 0.0), axis=0, keepdims=True) - 1.0).astype(jnp.int32))
    return items


def kernel(n_dp, n_table, *refs):
    names = INPUTS + OUTPUTS + tuple(scratch(n_dp, n_table))
    ns = type("Refs", (), dict(zip(names, refs)))
    dp, table = lax.axis_index("dp"), lax.axis_index("table")
    core = lax.rem(dp, 2)
    pairs = n_dp * n_table
    cap = SLOTS // pairs
    nx = 4
    ny = n_table // nx
    row_share, col_share, half_dp = D // n_table, D // n_dp, n_dp // 2
    x_rows = ny * row_share

    loads = {}
    for n, name in enumerate(INPUTS):
        held = getattr(ns, name + "_v")
        held = held.at[pl.ds(0, D)] if name == "w_in" else held
        loads[name] = pltpu.make_async_copy(getattr(ns, name), held, ns.load.at[n])
        loads[name].start()

    barrier = pltpu.get_barrier_semaphore()
    for axis, size, me in (("table", n_table, table), ("dp", n_dp, dp)):
        def greet(k, carry, axis=axis, size=size, me=me):
            pl.semaphore_signal(
                barrier, inc=1, device_id={axis: lax.rem(me + k, size)}, device_id_type=MESH
            )
            return carry
        lax.fori_loop(1, size, greet, 0)

    loads["lengths"].wait()
    build_bias(ns.lengths_v, ns.bias)
    loads["events"].wait()
    normalize_events(ns.events_v, ns.xnt, ns.normedt, ns.inv)
    loads["owners"].wait()
    loads["items"].wait()
    route_slots(ns.owners_v, ns.items_v, n_dp, n_table, ns.oh_a, ns.oh_b, ns.item_send)
    loads["w_in"].wait()
    project(ns.w_in_v, ns.normedt, ns.slope, ns.act, ns.half)
    sum_rows(ns.w_in_v)

    for h in range(HEADS):
        attend_head(h, ns.act, ns.bias, ns.w, ns.dsl, ns.att)
    norm_att(ns.att, ns.ainv, ns.act, ns.gated)
    loads["upstream"].wait()
    for half in range(2):
        ns.part[half] = dot_nn(ns.gated[...], ns.upstream_v[:, half * 256:half * 256 + 256])
    pl.semaphore_wait(barrier, n_table + n_dp - 2)
    start_all("table", n_table, 1, ns.item_send, ns.item_land, ns.send.at[0], ns.recv.at[0])
    to_core = pltpu.make_async_remote_copy(
        src_ref=ns.part.at[1 - core],
        dst_ref=ns.other,
        send_sem=ns.send.at[2],
        recv_sem=ns.recv.at[2],
        device_id={"dp": dp + 1 - 2 * core},
        device_id_type=MESH,
    )
    to_core.start()
    loads["w_out"].wait()
    ns.dot[...] = jnp.zeros_like(ns.dot)
    z_refs = (ns.slope, ns.half, ns.zg, ns.dot)
    att_backward(ns.w_out_v, ns.upstream_v, ns.upt, ns.att, ns.ainv, ns.act, ns.ag, z_refs)
    for h in range(HEADS):
        backward_head(h, ns.act, ns.ag, ns.w, ns.dsl, ns.ds, z_refs)
        if h == 5:
            to_core.wait_recv()
            for t in range(n_table):
                y, x = t // nx, t % nx
                rows = slice(t * row_share, (t + 1) * row_share)
                ns.x_send[x * x_rows + y * row_share:x * x_rows + (y + 1) * row_share] = (
                    ns.part[core, rows] + ns.other[rows]
                ).astype(BF16)
            start_all("table", nx, x_rows, ns.x_send, ns.x_recv, ns.send.at[3], ns.recv.at[3], lo=lax.div(table, nx) * nx)

    first = (("table", n_table, n_dp * cap), ("dp", n_dp, n_table * cap))
    second = first[::-1]

    def hop_one(path, half):
        lanes = pl.ds(half * 128, 128)
        start_all(
            *first[path], ns.moved.at[path, :, lanes], ns.landed.at[path, half],
            ns.hop_send.at[path, half, 0], ns.hop_recv.at[path, half, 0],
        )

    def hop_two(path, half):
        swap = (ns.swap_a, ns.swap_b)[path]
        wait_bytes(ns.landed.at[path, half], ns.hop_recv.at[path, half, 0])
        ns.again[path, half] = dot_nn(swap[...], ns.landed[path, half]).astype(BF16)
        start_all(
            *second[path], ns.again.at[path, half], ns.arrived.at[path, :, pl.ds(half * 128, 128)],
            ns.hop_send.at[path, half, 1], ns.hop_recv.at[path, half, 1],
        )

    for part in (1, 0):
        grad = event_gradient(part, ns.w_in_v, ns.zg, ns.dot, ns.stat, ns.upt, ns.xnt, ns.inv)
        for path, slots in ((0, ns.oh_a), (1, ns.oh_b)):
            lo = 128 if path != part else 0
            ns.moved[path, :, part * 128:part * 128 + 128] = dot_nt(slots[...], grad[lo:lo + 128]).astype(BF16)
            hop_one(path, part)

    wait_bytes(ns.item_land, ns.recv.at[0])
    ns.item_again[...] = turn_items(ns.item_land[...], n_dp, cap)
    start_all("dp", n_dp, 1, ns.item_again, ns.item_done, ns.send.at[1], ns.recv.at[1])
    ns.swap_a[...] = swap_rows(n_table, n_dp, cap)
    ns.swap_b[...] = swap_rows(n_dp, n_table, cap)

    wait_bytes(ns.x_recv, ns.recv.at[3])
    share = ns.x_recv[0:x_rows].astype(F32)
    for x in range(1, nx):
        share = share + ns.x_recv[x * x_rows:(x + 1) * x_rows].astype(F32)
    ns.y_send[...] = share.astype(BF16)
    start_all("table", ny, row_share, ns.y_send, ns.y_recv, ns.send.at[4], ns.recv.at[4], lo=lax.rem(table, nx), step=nx)

    hop_two(0, 1)
    hop_two(1, 1)

    hop_two(0, 0)
    hop_two(1, 0)

    wait_bytes(ns.y_recv, ns.recv.at[4])
    share = ns.y_recv[0:row_share].astype(F32)
    for y in range(1, ny):
        share = share + ns.y_recv[y * row_share:(y + 1) * row_share].astype(F32)
    for m in range(half_dp):
        cols = share[:, m * col_share:(m + 1) * col_share]
        if col_share < 128:
            cols = jnp.concatenate([cols, jnp.zeros((row_share, 128 - col_share), F32)], axis=1)
        ns.fin_send[m] = cols
    z = lax.div(dp, 2)
    for m in range(half_dp):
        target = core * half_dp + m
        group = ns.fin_send.at[m]

        @pl.when(target == dp)
        def _():
            pltpu.make_async_copy(group, ns.grad_parts.at[z], ns.recv.at[5]).start()

        @pl.when(target != dp)
        def _():
            pltpu.make_async_remote_copy(
                src_ref=group,
                dst_ref=ns.grad_parts.at[z],
                send_sem=ns.fin_sem.at[m],
                recv_sem=ns.recv.at[5],
                device_id={"dp": target},
                device_id_type=MESH,
            ).start()

    wait_bytes(ns.item_done, ns.recv.at[1])
    items = item_lanes(ns.item_done[...], n_dp, n_table)
    ns.item_rows_v[0:1, :] = items[0]
    ns.item_rows_v[1:2, :] = items[1]
    keep_items = pltpu.make_async_copy(ns.item_rows_v, ns.item_rows, ns.keep)
    keep_items.start()

    keep_items.wait()
    wait_bytes(ns.item_send.at[pl.ds(0, n_table - 1)], ns.send.at[0])
    wait_bytes(ns.item_again.at[pl.ds(0, n_dp - 1)], ns.send.at[1])
    to_core.wait_send()
    wait_bytes(ns.x_send.at[pl.ds(0, (nx - 1) * x_rows)], ns.send.at[3])
    if ny > 1:
        wait_bytes(ns.y_send.at[pl.ds(0, (ny - 1) * row_share)], ns.send.at[4])
    for m in range(half_dp):
        target = core * half_dp + m

        @pl.when(target != dp)
        def _():
            wait_bytes(ns.fin_send.at[m], ns.fin_sem.at[m])
    for half in range(2):
        for path in range(2):
            for hop, (_, size, rows) in enumerate((first[path], second[path])):
                wait_bytes(ns.again.at[path, half, pl.ds(0, (size - 1) * rows)], ns.hop_send.at[path, half, hop])
    for half in range(2):
        for path in range(2):
            wait_bytes(ns.arrived.at[path, :, pl.ds(half * 128, 128)], ns.hop_recv.at[path, half, 1])
    wait_bytes(ns.grad_parts, ns.recv.at[5])


def place_kernel(parts_ref, item_ref, arrived_ref, out_ref, table_ref, parts, items, rows, block, built, load, store):
    copies = [pltpu.make_async_copy(item_ref, items, load.at[2])]
    copies += [pltpu.make_async_copy(arrived_ref.at[p], rows.at[p], load.at[p]) for p in range(2)]
    copies += [pltpu.make_async_copy(parts_ref, parts, load.at[3])]
    for copy in copies:
        copy.start()
    copies[0].wait()
    blocks = built.shape[0]
    size = ROWS_DEV // blocks
    stores = []
    for b in range(blocks):
        for p in range(2):
            hits = one_hot(size, items[p:p + 1, :] - b * size)
            if b == 0:
                copies[p + 1].wait()
            placed = dot_nn(hits, rows[p]).astype(BF16)
            low, high = (0, 384) if p == 0 else (128, 256)
            built[b, :, low:low + 128] = placed[:, 0:128]
            built[b, :, high:high + 128] = placed[:, 128:256]
        stores.append(pltpu.make_async_copy(built.at[b], table_ref.at[pl.ds(b * size, size)], store.at[b]))
        stores[-1].start()
        if b == 0:
            copies[3].wait()
            total = parts[0]
            for k in range(1, parts.shape[0]):
                total = total + parts[k]
            block[...] = total[:, 0:block.shape[1]]
            stores.append(pltpu.make_async_copy(block, out_ref, store.at[blocks]))
            stores[-1].start()
    for copy in stores:
        copy.wait()


INPUTS = ("events", "lengths", "owners", "items", "w_in", "upstream", "w_out")
OUTPUTS = ("grad_parts", "item_rows", "arrived")


def scratch(n_dp, n_table):
    row_share = D // n_table
    item_lane = max(128, SLOTS // min(n_dp, n_table))
    vmem = pltpu.VMEM
    dma = pltpu.SemaphoreType.DMA
    return dict(
        events_v=vmem((TOK, D), BF16),
        lengths_v=vmem((1, 8), jnp.int32),
        owners_v=vmem((1, TOK), jnp.int32),
        items_v=vmem((1, TOK), jnp.int32),
        upstream_v=vmem((TOK, D), BF16),
        w_in_v=vmem((D + 16, 4 * D), BF16),
        half=vmem((4 * D, TOK), F32),
        upt=vmem((D, TOK), BF16),
        dot=vmem((1, TOK), F32),
        stat=vmem((8, TOK), F32),
        w_out_v=vmem((D, D), BF16),
        bias=vmem((TOK, TOK), F32),
        xnt=vmem((D, TOK), F32),
        normedt=vmem((D, TOK), BF16),
        inv=vmem((1, TOK), F32),
        slope=vmem((4 * D, TOK), F32),
        act=vmem((4 * D, TOK), BF16),
        w=vmem((HEADS, TOK, TOK), BF16),
        dsl=vmem((HEADS, TOK, TOK), F32),
        att=vmem((D, TOK), F32),
        ainv=vmem((1, TOK), F32),
        gated=vmem((D, TOK), BF16),
        zg=vmem((4 * D, TOK), BF16),
        ag=vmem((D, TOK), BF16),
        ds=vmem((TOK, TOK), BF16),
        oh_a=vmem((SLOTS, TOK), BF16),
        oh_b=vmem((SLOTS, TOK), BF16),
        swap_a=vmem((SLOTS, SLOTS), BF16),
        swap_b=vmem((SLOTS, SLOTS), BF16),
        item_send=vmem((n_table, item_lane), F32),
        item_land=vmem((n_table, item_lane), F32),
        item_again=vmem((n_dp, item_lane), F32),
        item_done=vmem((n_dp, item_lane), F32),
        moved=vmem((2, SLOTS, 256), BF16),
        landed=vmem((2, 2, SLOTS, 128), BF16),
        again=vmem((2, 2, SLOTS, 128), BF16),
        part=vmem((2, D, 256), F32),
        other=vmem((D, 256), F32),
        x_send=vmem((D, 256), BF16),
        x_recv=vmem((D, 256), BF16),
        y_send=vmem((D // 4, 256), BF16),
        y_recv=vmem((D // 4, 256), BF16),
        fin_send=vmem((n_dp // 2, row_share, 128), F32),
        item_rows_v=vmem((8, SLOTS), jnp.int32),
        load=dma((len(INPUTS),)),
        keep=dma(()),
        send=dma((6,)),
        recv=dma((6,)),
        hop_send=dma((2, 2, 2)),
        hop_recv=dma((2, 2, 2)),
        fin_sem=dma((n_dp // 2,)),
    )


def solution(mesh):
    n_dp, n_table = mesh.shape["dp"], mesh.shape["table"]
    anywhere = pl.BlockSpec(memory_space=pl.ANY)

    def local(events, upstream, w_in, w_out, lengths, owners, item_rows):
        row_share, col_share = D // n_table, D // n_dp
        exchanged = pl.pallas_call(
            functools.partial(kernel, n_dp, n_table),
            out_shape=(
                jax.ShapeDtypeStruct((n_dp // 2, row_share, 128), F32),
                jax.ShapeDtypeStruct((8, SLOTS), jnp.int32),
                jax.ShapeDtypeStruct((2, SLOTS, 256), BF16),
            ),
            in_specs=[anywhere] * len(INPUTS),
            out_specs=[anywhere] * 3,
            scratch_shapes=list(scratch(n_dp, n_table).values()),
            compiler_params=pltpu.CompilerParams(
                collective_id=0, has_side_effects=True, vmem_limit_bytes=60 << 20
            ),
        )(events, lengths, owners.reshape(1, TOK), item_rows.reshape(1, TOK), w_in, upstream, w_out)
        return pl.pallas_call(
            place_kernel,
            out_shape=(
                jax.ShapeDtypeStruct((row_share, col_share), F32),
                jax.ShapeDtypeStruct((ROWS_DEV, D), BF16),
            ),
            in_specs=[anywhere] * 3,
            out_specs=(anywhere, anywhere),
            scratch_shapes=[
                pltpu.VMEM((n_dp // 2, row_share, 128), F32),
                pltpu.VMEM((8, SLOTS), jnp.int32),
                pltpu.VMEM((2, SLOTS, 256), BF16),
                pltpu.VMEM((row_share, col_share), F32),
                pltpu.VMEM((PLACE_BLOCKS, ROWS_DEV // PLACE_BLOCKS, D), BF16),
                pltpu.SemaphoreType.DMA((4,)),
                pltpu.SemaphoreType.DMA((PLACE_BLOCKS + 1,)),
            ],
            compiler_params=pltpu.CompilerParams(vmem_limit_bytes=60 << 20),
        )(*exchanged)

    both = P(("dp", "table"), None)
    return jax.shard_map(
        local,
        mesh=mesh,
        in_specs=(both, both, P(), P(), both, both, P(("dp", "table"))),
        out_specs=(P("table", "dp"), both),
        check_vma=False,
    )
```

```python
import functools
import jax
import jax.numpy as jnp
from jax import lax
from jax.experimental import pallas as pl
from jax.experimental.pallas import tpu as pltpu
from jax.sharding import PartitionSpec as P

HEADS = 8
HD = 64
TOK = 512
D = 512
EPS = 1e-6
F32 = jnp.float32
BF16 = jnp.bfloat16
JB = 256
OUT_OF_MASK = -1e30


def dot_nn(a, b):
    return lax.dot_general(a, b, (((1,), (0,)), ((), ())), preferred_element_type=F32)


def dot_nt(a, b):
    return lax.dot_general(a, b, (((1,), (1,)), ((), ())), preferred_element_type=F32)


def window(jb):
    lo = jb * JB
    return lo, min(TOK, -(-(lo + JB + 255) // 128) * 128)


def build_bias(len_ref, bias_ref):
    lengths = len_ref[...]
    upto = lax.broadcasted_iota(jnp.int32, (8, 8), 1) <= lax.broadcasted_iota(jnp.int32, (8, 8), 0)
    ends = jnp.sum(jnp.where(upto, lengths.astype(F32), 0.0), axis=1, keepdims=True).astype(jnp.int32)
    col = lax.broadcasted_iota(jnp.int32, (TOK, 1), 0)
    row = lax.broadcasted_iota(jnp.int32, (1, TOK), 1)
    seg_row = jnp.sum(jnp.where(row >= ends, 1.0, 0.0), axis=0, keepdims=True)
    seg_col = jnp.broadcast_to(seg_row, (128, TOK)).T[:, 0:1]
    for jb in range(TOK // JB):
        lo, hi = window(jb)
        keep = (seg_col[lo:lo + JB] == seg_row[:, lo:hi]) & (col[lo:lo + JB] <= row[:, lo:hi])
        bias_ref[lo:lo + JB, lo:hi] = jnp.where(keep, 0.0, OUT_OF_MASK)


def normalize_events(ev_ref, xnt_ref, normedt_ref, inv_ref):
    x = ev_ref[...].T.astype(F32)
    mean = jnp.mean(x, axis=0, keepdims=True)
    c = x - mean
    inv = lax.rsqrt(jnp.mean(c * c, axis=0, keepdims=True) + EPS)
    xn = c * inv
    xnt_ref[...] = xn
    normedt_ref[...] = xn.astype(BF16)
    inv_ref[...] = inv


def project(w_in_ref, normedt_ref, slope_ref, act_ref, half_ref):
    for c in range(16):
        lo = c * 128
        wt = w_in_ref[0:D, lo:lo + 128].T
        half = dot_nn(wt, normedt_ref[...]) * 0.5
        half_ref[lo:lo + 128, :] = half
        t = jnp.tanh(half)
        p = 1.0 + t
        act = half * p
        slope_ref[lo:lo + 128, :] = p + act * (1.0 - t)
        act_ref[lo:lo + 128, :] = act.astype(BF16)


def natural(act_ref, nat_ref):
    nat_ref[:, 0:512] = act_ref[512:1024, :].T
    nat_ref[:, 512:1024] = act_ref[1536:2048, :].T


def head_pair_cols(nat_ref, base, pair):
    return nat_ref[:, pl.ds(pl.multiple_of(base + pair * 128, 128), 128)]


def attend_head(h, act_ref, bias_ref, w_ref, dsl_ref, att_ref):
    r = pl.multiple_of(h * HD, HD)
    qt = act_ref[pl.ds(1024 + r, HD), :] * 0.0625
    kt = act_ref[pl.ds(1536 + r, HD), :]
    vt = act_ref[pl.ds(512 + r, HD), :] * (1.0 / 64.0)
    k = kt.T
    for jb in range(TOK // JB):
        lo, hi = window(jb)
        half = dot_nn(k[lo:lo + JB], qt[:, lo:hi]) + bias_ref[lo:lo + JB, lo:hi]
        t = jnp.tanh(half)
        p = 1.0 + t
        w = half * p
        w_ref[h, lo:lo + JB, lo:hi] = w.astype(BF16)
        dsl_ref[h, lo:lo + JB, lo:hi] = p + w * (1.0 - t)
    att_ref[pl.ds(r, HD), 0:256] = dot_nn(vt[:, 0:256], w_ref[h, 0:256, 0:256])
    att_ref[pl.ds(r, HD), 256:512] = dot_nn(vt, w_ref[h, :, 256:512])


def norm_att(att_ref, ainv_ref, act_ref, gated_ref):
    a = att_ref[...]
    mean = jnp.mean(a, axis=0, keepdims=True)
    c = a - mean
    inv = lax.rsqrt(jnp.mean(c * c, axis=0, keepdims=True) + EPS)
    an = c * inv
    att_ref[...] = an
    ainv_ref[...] = inv
    gated_ref[...] = (an * act_ref[0:512, :].astype(F32)).astype(BF16)


def put_z_grad(at, lanes, joined, slope_ref, half_ref, zg_ref, dot_ref):
    grad = (joined * slope_ref[at, lanes]).astype(BF16)
    zg_ref[at, lanes] = grad
    dot_ref[:, lanes] += jnp.sum(grad.astype(F32) * half_ref[at, lanes], axis=0, keepdims=True)


def att_backward(w_out_ref, up_ref, upt_ref, att_ref, ainv_ref, act_ref, ag_ref, z_refs):
    upt_ref[...] = up_ref[...].T
    gg = dot_nn(w_out_ref[...], upt_ref[...])
    an = att_ref[...]
    put_z_grad(slice(0, 512), slice(0, 512), gg * an, *z_refs)
    g = gg * act_ref[0:512, :].astype(F32)
    first = jnp.mean(g, axis=0, keepdims=True)
    second = jnp.mean(g * an, axis=0, keepdims=True)
    ag_ref[...] = ((g - first - an * second) * (ainv_ref[...] * (1.0 / 128.0))).astype(BF16)


def backward_head(h, act_ref, ag_ref, w_ref, dsl_ref, ds_ref, z_refs):
    r = h * HD
    qt = act_ref[1024 + r:1024 + r + HD, :]
    kt = act_ref[1536 + r:1536 + r + HD, :]
    v = act_ref[512 + r:512 + r + HD, :].T
    ag = ag_ref[r:r + HD, :]
    for jb in range(TOK // JB):
        lo, hi = window(jb)
        wg = dot_nn(v[lo:lo + JB], ag[:, lo:hi])
        ds_ref[lo:lo + JB, lo:hi] = (wg * dsl_ref[h, lo:lo + JB, lo:hi]).astype(BF16)
    left, right = slice(0, 256), slice(256, 512)
    rows = [slice(base + r, base + r + HD) for base in (512, 1024, 1536)]
    put_z_grad(rows[0], left, dot_nt(ag, w_ref[h, 0:256, :]) * 2.0, *z_refs)
    put_z_grad(rows[0], right, dot_nt(ag[:, right], w_ref[h, right, right]) * 2.0, *z_refs)
    put_z_grad(rows[1], left, dot_nn(kt[:, left], ds_ref[left, left]) * 0.125, *z_refs)
    put_z_grad(rows[1], right, dot_nn(kt, ds_ref[:, right]) * 0.125, *z_refs)
    put_z_grad(rows[2], left, dot_nt(qt, ds_ref[left, :]) * 0.125, *z_refs)
    put_z_grad(rows[2], right, dot_nt(qt[:, right], ds_ref[right, right]) * 0.125, *z_refs)


def sum_rows(w_in_ref):
    sums = dot_nn(jnp.ones((8, D), BF16), w_in_ref[0:D, :])
    high = sums.astype(BF16)
    w_in_ref[D:D + 16, :] = jnp.concatenate([high, (sums - high.astype(F32)).astype(BF16)], axis=0)


def event_gradient(part, w_in_ref, zg_ref, dot_ref, stat_ref, upt_ref, xnt_ref, inv_ref):
    if part == 1:
        at = slice(256, 512)
        ng = dot_nn(w_in_ref[256:D + 16, :], zg_ref[...])
        stat_ref[0:1, :] = (ng[256:257] + ng[264:265]) * (1.0 / 512.0)
        stat_ref[1:2, :] = dot_ref[...] * (1.0 / 256.0)
        ng = ng[0:256]
    else:
        at = slice(0, 256)
        ng = dot_nn(w_in_ref[at, :], zg_ref[...])
    back = (ng - stat_ref[0:1, :] - xnt_ref[at, :] * stat_ref[1:2, :]) * (inv_ref[...] * 0.5)
    return (upt_ref[at, :].astype(F32) + back).astype(BF16)


MESH = pl.DeviceIdType.MESH
SLOTS = 1024
ROWS_DEV = 1024
PLACE_BLOCKS = 8


def log2(n):
    return n.bit_length() - 1


def one_hot(rows, cols_of):
    at = lax.broadcasted_iota(jnp.int32, (rows, cols_of.shape[1]), 0)
    return jnp.where(at == cols_of, 1.0, 0.0).astype(BF16)


def block_at(n, rows):
    return pl.ds(pl.multiple_of(n * rows, rows), rows) if rows > 1 else pl.ds(n, 1)


def start_all(axis, size, rows, src_ref, dst_ref, send_sem, recv_sem, lo=0, step=1):
    at = lax.axis_index(axis)
    me = lax.div(at - lo, step)
    mine = block_at(me, rows)
    pltpu.make_async_copy(src_ref.at[mine], dst_ref.at[mine], recv_sem).start()

    def send(k, carry):
        peer = lax.rem(me + k, size)
        pltpu.make_async_remote_copy(
            src_ref=src_ref.at[block_at(peer, rows)],
            dst_ref=dst_ref.at[mine],
            send_sem=send_sem,
            recv_sem=recv_sem,
            device_id={axis: lo + peer * step},
            device_id_type=MESH,
        ).start()
        return carry

    lax.fori_loop(1, size, send, 0)


def wait_bytes(ref, sem):
    pltpu.make_async_copy(ref, ref, sem).wait()


def route_slots(owner_ref, item_ref, n_dp, n_table, oh_a, oh_b, meta_ref):
    pairs = n_dp * n_table
    cap = SLOTS // pairs
    row = owner_ref[...]
    col = jnp.broadcast_to(row, (128, TOK)).T[:, 0:1]
    place_col = lax.broadcasted_iota(jnp.int32, (TOK, 1), 0)
    place_row = lax.broadcasted_iota(jnp.int32, (1, TOK), 1)
    earlier = (col == row) & (place_col < place_row)
    rank = jnp.sum(jnp.where(earlier, 1.0, 0.0), axis=0, keepdims=True).astype(jnp.int32)
    table, dp = row & (n_table - 1), row >> log2(n_table)
    oh_a[...] = one_hot(SLOTS, table * (n_dp * cap) + dp * cap + rank)
    oh_b[...] = one_hot(SLOTS, dp * (n_table * cap) + table * cap + rank)
    code = item_ref[...] + 1
    to_table = one_hot(n_table, table).astype(F32)
    lane = one_hot(meta_ref.shape[1], dp * cap + rank)
    high, low = (dot_nt((to_table * word.astype(F32)).astype(BF16), lane) for word in (code >> 5, code & 31))
    meta_ref[...] = high * 32.0 + low


def words(values):
    whole = values.astype(jnp.int32)
    return (whole >> 5).astype(F32).astype(BF16), (whole & 31).astype(F32).astype(BF16)


def turn_items(landed, n_dp, cap):
    n_table, lanes = landed.shape
    row = lax.broadcasted_iota(jnp.int32, (lanes, 1), 0)
    col = lax.broadcasted_iota(jnp.int32, (1, lanes), 1)
    spread = one_hot(n_table, col >> log2(cap))
    gather = jnp.where((lax.broadcasted_iota(jnp.int32, (n_dp, lanes), 0)) == (
        lax.broadcasted_iota(jnp.int32, (n_dp, lanes), 1) >> log2(cap)), 1.0, 0.0).astype(BF16)
    parts = []
    for word in words(landed):
        turned = dot_nn(word.astype(F32).T.astype(BF16), spread)
        kept = jnp.where((row & (cap - 1)) == (col & (cap - 1)), turned, 0.0).astype(BF16)
        parts.append(dot_nn(gather, kept))
    return parts[0] * 32.0 + parts[1]


def swap_rows(first, second, cap):
    n = first * second * cap
    out = lax.broadcasted_iota(jnp.int32, (n, 1), 0)
    slot = out & (cap - 1)
    a = (out >> log2(cap)) & (first - 1)
    b = out >> (log2(cap) + log2(first))
    at = lax.broadcasted_iota(jnp.int32, (n, n), 1)
    return jnp.where(at == a * (second * cap) + b * cap + slot, 1.0, 0.0).astype(BF16)


def item_lanes(turned, n_dp, n_table):
    cap = SLOTS // (n_dp * n_table)
    col = lax.broadcasted_iota(jnp.int32, (1, SLOTS), 1)
    row = lax.broadcasted_iota(jnp.int32, (n_dp, SLOTS), 0)
    slot, pair = col & (cap - 1), col >> log2(cap)
    high, low = words(turned)
    items = []
    for dp, table in ((pair >> log2(n_table), pair & (n_table - 1)), (pair & (n_dp - 1), pair >> log2(n_dp))):
        spread = one_hot(turned.shape[1], table * cap + slot)
        every = dot_nn(high, spread) * 32.0 + dot_nn(low, spread)
        items.append((jnp.sum(jnp.where(row == dp, every, 0.0), axis=0, keepdims=True) - 1.0).astype(jnp.int32))
    return items


def kernel(n_dp, n_table, *refs):
    names = INPUTS + OUTPUTS + tuple(scratch(n_dp, n_table))
    ns = type("Refs", (), dict(zip(names, refs)))
    dp, table = lax.axis_index("dp"), lax.axis_index("table")
    core = lax.rem(dp, 2)
    pairs = n_dp * n_table
    cap = SLOTS // pairs
    nx = 4
    ny = n_table // nx
    row_share, col_share, half_dp = D // n_table, D // n_dp, n_dp // 2
    x_rows = ny * row_share

    loads = {}
    for n, name in enumerate(INPUTS):
        held = getattr(ns, name + "_v")
        held = held.at[pl.ds(0, D)] if name == "w_in" else held
        loads[name] = pltpu.make_async_copy(getattr(ns, name), held, ns.load.at[n])
        loads[name].start()

    barrier = pltpu.get_barrier_semaphore()
    for axis, size, me in (("table", n_table, table), ("dp", n_dp, dp)):
        def greet(k, carry, axis=axis, size=size, me=me):
            pl.semaphore_signal(
                barrier, inc=1, device_id={axis: lax.rem(me + k, size)}, device_id_type=MESH
            )
            return carry
        lax.fori_loop(1, size, greet, 0)

    loads["lengths"].wait()
    build_bias(ns.lengths_v, ns.bias)
    loads["events"].wait()
    normalize_events(ns.events_v, ns.xnt, ns.normedt, ns.inv)
    loads["owners"].wait()
    loads["items"].wait()
    route_slots(ns.owners_v, ns.items_v, n_dp, n_table, ns.oh_a, ns.oh_b, ns.item_send)
    loads["w_in"].wait()
    project(ns.w_in_v, ns.normedt, ns.slope, ns.act, ns.half)
    sum_rows(ns.w_in_v)

    for h in range(HEADS):
        attend_head(h, ns.act, ns.bias, ns.w, ns.dsl, ns.att)
    norm_att(ns.att, ns.ainv, ns.act, ns.gated)
    loads["upstream"].wait()
    for half in range(2):
        ns.part[half] = dot_nn(ns.gated[...], ns.upstream_v[:, half * 256:half * 256 + 256])
    pl.semaphore_wait(barrier, n_table + n_dp - 2)
    start_all("table", n_table, 1, ns.item_send, ns.item_land, ns.send.at[0], ns.recv.at[0])
    to_core = pltpu.make_async_remote_copy(
        src_ref=ns.part.at[1 - core],
        dst_ref=ns.other,
        send_sem=ns.send.at[2],
        recv_sem=ns.recv.at[2],
        device_id={"dp": dp + 1 - 2 * core},
        device_id_type=MESH,
    )
    to_core.start()
    loads["w_out"].wait()
    ns.dot[...] = jnp.zeros_like(ns.dot)
    z_refs = (ns.slope, ns.half, ns.zg, ns.dot)
    att_backward(ns.w_out_v, ns.upstream_v, ns.upt, ns.att, ns.ainv, ns.act, ns.ag, z_refs)
    for h in range(HEADS):
        backward_head(h, ns.act, ns.ag, ns.w, ns.dsl, ns.ds, z_refs)
    to_core.wait_recv()
    for t in range(n_table):
        y, x = t // nx, t % nx
        rows = slice(t * row_share, (t + 1) * row_share)
        ns.x_send[x * x_rows + y * row_share:x * x_rows + (y + 1) * row_share] = (
            ns.part[core, rows] + ns.other[rows]
        ).astype(BF16)
    start_all("table", nx, x_rows, ns.x_send, ns.x_recv, ns.send.at[3], ns.recv.at[3], lo=lax.div(table, nx) * nx)

    first = (("table", n_table, n_dp * cap), ("dp", n_dp, n_table * cap))
    second = first[::-1]

    def hop_one(path, half):
        lanes = pl.ds(half * 128, 128)
        start_all(
            *first[path], ns.moved.at[path, :, lanes], ns.landed.at[path, half],
            ns.hop_send.at[path, half, 0], ns.hop_recv.at[path, half, 0],
        )

    def hop_two(path, half):
        swap = (ns.swap_a, ns.swap_b)[path]
        wait_bytes(ns.landed.at[path, half], ns.hop_recv.at[path, half, 0])
        ns.again[path, half] = dot_nn(swap[...], ns.landed[path, half]).astype(BF16)
        start_all(
            *second[path], ns.again.at[path, half], ns.arrived.at[path, :, pl.ds(half * 128, 128)],
            ns.hop_send.at[path, half, 1], ns.hop_recv.at[path, half, 1],
        )

    for part in (1, 0):
        grad = event_gradient(part, ns.w_in_v, ns.zg, ns.dot, ns.stat, ns.upt, ns.xnt, ns.inv)
        for path, slots in ((0, ns.oh_a), (1, ns.oh_b)):
            lo = 128 if path != part else 0
            ns.moved[path, :, part * 128:part * 128 + 128] = dot_nt(slots[...], grad[lo:lo + 128]).astype(BF16)
            hop_one(path, part)

    wait_bytes(ns.item_land, ns.recv.at[0])
    ns.item_again[...] = turn_items(ns.item_land[...], n_dp, cap)
    start_all("dp", n_dp, 1, ns.item_again, ns.item_done, ns.send.at[1], ns.recv.at[1])
    ns.swap_a[...] = swap_rows(n_table, n_dp, cap)
    ns.swap_b[...] = swap_rows(n_dp, n_table, cap)

    wait_bytes(ns.x_recv, ns.recv.at[3])
    share = ns.x_recv[0:x_rows].astype(F32)
    for x in range(1, nx):
        share = share + ns.x_recv[x * x_rows:(x + 1) * x_rows].astype(F32)
    ns.y_send[...] = share.astype(BF16)
    start_all("table", ny, row_share, ns.y_send, ns.y_recv, ns.send.at[4], ns.recv.at[4], lo=lax.rem(table, nx), step=nx)

    hop_two(0, 1)
    hop_two(1, 1)

    hop_two(0, 0)
    hop_two(1, 0)

    wait_bytes(ns.y_recv, ns.recv.at[4])
    share = ns.y_recv[0:row_share].astype(F32)
    for y in range(1, ny):
        share = share + ns.y_recv[y * row_share:(y + 1) * row_share].astype(F32)
    for m in range(half_dp):
        cols = share[:, m * col_share:(m + 1) * col_share]
        if col_share < 128:
            cols = jnp.concatenate([cols, jnp.zeros((row_share, 128 - col_share), F32)], axis=1)
        ns.fin_send[m] = cols
    z = lax.div(dp, 2)
    for m in range(half_dp):
        target = core * half_dp + m
        group = ns.fin_send.at[m]

        @pl.when(target == dp)
        def _():
            pltpu.make_async_copy(group, ns.grad_parts.at[z], ns.recv.at[5]).start()

        @pl.when(target != dp)
        def _():
            pltpu.make_async_remote_copy(
                src_ref=group,
                dst_ref=ns.grad_parts.at[z],
                send_sem=ns.fin_sem.at[m],
                recv_sem=ns.recv.at[5],
                device_id={"dp": target},
                device_id_type=MESH,
            ).start()

    wait_bytes(ns.item_done, ns.recv.at[1])
    items = item_lanes(ns.item_done[...], n_dp, n_table)
    ns.item_rows_v[0:1, :] = items[0]
    ns.item_rows_v[1:2, :] = items[1]
    keep_items = pltpu.make_async_copy(ns.item_rows_v, ns.item_rows, ns.keep)
    keep_items.start()

    keep_items.wait()
    wait_bytes(ns.item_send.at[pl.ds(0, n_table - 1)], ns.send.at[0])
    wait_bytes(ns.item_again.at[pl.ds(0, n_dp - 1)], ns.send.at[1])
    to_core.wait_send()
    wait_bytes(ns.x_send.at[pl.ds(0, (nx - 1) * x_rows)], ns.send.at[3])
    if ny > 1:
        wait_bytes(ns.y_send.at[pl.ds(0, (ny - 1) * row_share)], ns.send.at[4])
    for m in range(half_dp):
        target = core * half_dp + m

        @pl.when(target != dp)
        def _():
            wait_bytes(ns.fin_send.at[m], ns.fin_sem.at[m])
    for half in range(2):
        for path in range(2):
            for hop, (_, size, rows) in enumerate((first[path], second[path])):
                wait_bytes(ns.again.at[path, half, pl.ds(0, (size - 1) * rows)], ns.hop_send.at[path, half, hop])
    for half in range(2):
        for path in range(2):
            wait_bytes(ns.arrived.at[path, :, pl.ds(half * 128, 128)], ns.hop_recv.at[path, half, 1])
    wait_bytes(ns.grad_parts, ns.recv.at[5])


def place_kernel(parts_ref, item_ref, arrived_ref, out_ref, table_ref, parts, items, rows, block, built, load, store):
    copies = [pltpu.make_async_copy(item_ref, items, load.at[2])]
    copies += [pltpu.make_async_copy(arrived_ref.at[p], rows.at[p], load.at[p]) for p in range(2)]
    copies += [pltpu.make_async_copy(parts_ref, parts, load.at[3])]
    for copy in copies:
        copy.start()
    copies[0].wait()
    blocks = built.shape[0]
    size = ROWS_DEV // blocks
    stores = []
    for b in range(blocks):
        for p in range(2):
            hits = one_hot(size, items[p:p + 1, :] - b * size)
            if b == 0:
                copies[p + 1].wait()
            placed = dot_nn(hits, rows[p]).astype(BF16)
            low, high = (0, 384) if p == 0 else (128, 256)
            built[b, :, low:low + 128] = placed[:, 0:128]
            built[b, :, high:high + 128] = placed[:, 128:256]
        stores.append(pltpu.make_async_copy(built.at[b], table_ref.at[pl.ds(b * size, size)], store.at[b]))
        stores[-1].start()
        if b == 0:
            copies[3].wait()
            total = parts[0]
            for k in range(1, parts.shape[0]):
                total = total + parts[k]
            block[...] = total[:, 0:block.shape[1]]
            stores.append(pltpu.make_async_copy(block, out_ref, store.at[blocks]))
            stores[-1].start()
    for copy in stores:
        copy.wait()


INPUTS = ("events", "lengths", "owners", "items", "w_in", "upstream", "w_out")
OUTPUTS = ("grad_parts", "item_rows", "arrived")


def scratch(n_dp, n_table):
    row_share = D // n_table
    item_lane = max(128, SLOTS // min(n_dp, n_table))
    vmem = pltpu.VMEM
    dma = pltpu.SemaphoreType.DMA
    return dict(
        events_v=vmem((TOK, D), BF16),
        lengths_v=vmem((1, 8), jnp.int32),
        owners_v=vmem((1, TOK), jnp.int32),
        items_v=vmem((1, TOK), jnp.int32),
        upstream_v=vmem((TOK, D), BF16),
        w_in_v=vmem((D + 16, 4 * D), BF16),
        half=vmem((4 * D, TOK), F32),
        upt=vmem((D, TOK), BF16),
        dot=vmem((1, TOK), F32),
        stat=vmem((8, TOK), F32),
        w_out_v=vmem((D, D), BF16),
        bias=vmem((TOK, TOK), F32),
        xnt=vmem((D, TOK), F32),
        normedt=vmem((D, TOK), BF16),
        inv=vmem((1, TOK), F32),
        slope=vmem((4 * D, TOK), F32),
        act=vmem((4 * D, TOK), BF16),
        w=vmem((HEADS, TOK, TOK), BF16),
        dsl=vmem((HEADS, TOK, TOK), F32),
        att=vmem((D, TOK), F32),
        ainv=vmem((1, TOK), F32),
        gated=vmem((D, TOK), BF16),
        zg=vmem((4 * D, TOK), BF16),
        ag=vmem((D, TOK), BF16),
        ds=vmem((TOK, TOK), BF16),
        oh_a=vmem((SLOTS, TOK), BF16),
        oh_b=vmem((SLOTS, TOK), BF16),
        swap_a=vmem((SLOTS, SLOTS), BF16),
        swap_b=vmem((SLOTS, SLOTS), BF16),
        item_send=vmem((n_table, item_lane), F32),
        item_land=vmem((n_table, item_lane), F32),
        item_again=vmem((n_dp, item_lane), F32),
        item_done=vmem((n_dp, item_lane), F32),
        moved=vmem((2, SLOTS, 256), BF16),
        landed=vmem((2, 2, SLOTS, 128), BF16),
        again=vmem((2, 2, SLOTS, 128), BF16),
        part=vmem((2, D, 256), F32),
        other=vmem((D, 256), F32),
        x_send=vmem((D, 256), BF16),
        x_recv=vmem((D, 256), BF16),
        y_send=vmem((D // 4, 256), BF16),
        y_recv=vmem((D // 4, 256), BF16),
        fin_send=vmem((n_dp // 2, row_share, 128), F32),
        item_rows_v=vmem((8, SLOTS), jnp.int32),
        load=dma((len(INPUTS),)),
        keep=dma(()),
        send=dma((6,)),
        recv=dma((6,)),
        hop_send=dma((2, 2, 2)),
        hop_recv=dma((2, 2, 2)),
        fin_sem=dma((n_dp // 2,)),
    )


def solution(mesh):
    n_dp, n_table = mesh.shape["dp"], mesh.shape["table"]
    anywhere = pl.BlockSpec(memory_space=pl.ANY)

    def local(events, upstream, w_in, w_out, lengths, owners, item_rows):
        row_share, col_share = D // n_table, D // n_dp
        exchanged = pl.pallas_call(
            functools.partial(kernel, n_dp, n_table),
            out_shape=(
                jax.ShapeDtypeStruct((n_dp // 2, row_share, 128), F32),
                jax.ShapeDtypeStruct((8, SLOTS), jnp.int32),
                jax.ShapeDtypeStruct((2, SLOTS, 256), BF16),
            ),
            in_specs=[anywhere] * len(INPUTS),
            out_specs=[anywhere] * 3,
            scratch_shapes=list(scratch(n_dp, n_table).values()),
            compiler_params=pltpu.CompilerParams(
                collective_id=0, has_side_effects=True, vmem_limit_bytes=60 << 20
            ),
        )(events, lengths, owners.reshape(1, TOK), item_rows.reshape(1, TOK), w_in, upstream, w_out)
        return pl.pallas_call(
            place_kernel,
            out_shape=(
                jax.ShapeDtypeStruct((row_share, col_share), F32),
                jax.ShapeDtypeStruct((ROWS_DEV, D), BF16),
            ),
            in_specs=[anywhere] * 3,
            out_specs=(anywhere, anywhere),
            scratch_shapes=[
                pltpu.VMEM((n_dp // 2, row_share, 128), F32),
                pltpu.VMEM((8, SLOTS), jnp.int32),
                pltpu.VMEM((2, SLOTS, 256), BF16),
                pltpu.VMEM((row_share, col_share), F32),
                pltpu.VMEM((PLACE_BLOCKS, ROWS_DEV // PLACE_BLOCKS, D), BF16),
                pltpu.SemaphoreType.DMA((4,)),
                pltpu.SemaphoreType.DMA((PLACE_BLOCKS + 1,)),
            ],
            compiler_params=pltpu.CompilerParams(vmem_limit_bytes=60 << 20),
        )(*exchanged)

    both = P(("dp", "table"), None)
    return jax.shard_map(
        local,
        mesh=mesh,
        in_specs=(both, both, P(), P(), both, both, P(("dp", "table"))),
        out_specs=(P("table", "dp"), both),
        check_vma=False,
    )
```
